32 devices in a mesh: chan: 4 (over x, core), half: 2 (over y), ctx: 4 (over z).
Axes of the slice: x: 2, y: 2, z: 4, core: 2. Of those that a mesh axis runs over, the one named last changes fastest.
Arguments:
- query_gate: bfloat16 [2048, 8192], P('ctx', 'chan'), parts along dimension 1, may hold values from -6 to 6
- key_gate: bfloat16 [2048, 8192], P('ctx', 'chan'), parts along dimension 1, may hold values from -6 to 6
- value_input: bfloat16 [2048, 8192], P('ctx', 'chan'), parts along dimension 1, may hold values from -6 to 6
- residues: float32 [16, 8192], P(None, 'chan'), parts along dimension 1, may hold values from -1.5 to 1.5
- decays: float32 [16, 8192], P(None, 'chan'), parts along dimension 1, may hold values from 2.4414063e-05 to 0.05
- skip_gain: float32 [8192], P('chan'), parts along dimension 0, may hold values from 0.25 to 1
Outputs:
- mixed: bfloat16 [2048, 8192], P('ctx', 'chan'), parts along dimension 1
The draws below stay inside these ranges and needn't reach their ends.
There are 4 independent parts, one for each index of `chan`. The reference program is written for one: setup_inputs(seed, part) draws one part's arguments, and reference() takes and returns one part's arrays. A program takes and returns all parts, laid end to end along the dimension named above; each array names one. Nothing has to cross between parts.
All inputs are finite; a program needn't handle non-finite values.
Results may differ from the reference program's by a relative error of at most 0.00155.
Values may be sent and summed in bfloat16 or wider, within the bound.
No kernel may reach another device: no remote copies, remote signals or barrier semaphores. Data moves between devices by JAX's collectives and lax.ppermute only.
A program may use at most 128 MiB of HBM per device.

```python
import math
import jax
import jax.numpy as jnp

CHANNELS = 2048
MODES = 16
SEQ = 2048


def levels(stream_key, extent, shards, low, top_value):
    def one(position, blocks):
        steps = jax.random.uniform(jax.random.fold_in(jax.random.fold_in(stream_key, 6), position), (blocks,), jnp.float32, low / len(shards), top_value / len(shards))
        return jnp.repeat(jnp.exp(steps), extent[position] // blocks).reshape((-1,) + (1,) * (len(extent) - position - 1))

    level = one(*shards[0])
    for cut in shards[1:]:
        level = level * one(*cut)
    return level


def noise(stream_key, shape, deviation, most, cuts=(), kind=jnp.bfloat16):
    result = deviation * jax.random.normal(stream_key, shape, jnp.float32)
    if cuts:
        result = result * levels(stream_key, shape, cuts, -0.22, 0.18)
    return jnp.clip(result, -most, most).astype(kind)


def setup_inputs(seed: int = 0, part: int = 0) -> dict:
    keys = jax.random.split(jax.random.key(seed), 7)
    own_keys = jax.random.split(jax.random.fold_in(keys[6], part), 7)
    query_gate = noise(own_keys[0], (SEQ, CHANNELS), 1.0, 6.0, ((0, 4),))
    key_gate = noise(own_keys[1], (SEQ, CHANNELS), 1.0, 6.0, ((0, 4),))
    value_input = noise(own_keys[2], (SEQ, CHANNELS), 1.0, 6.0, ((0, 4),))
    residues = noise(own_keys[3], (MODES, CHANNELS), MODES ** -0.5, 1.5, (), jnp.float32)
    decays = jnp.clip(jnp.exp(jax.random.uniform(own_keys[4], (MODES, CHANNELS), jnp.float32, math.log(2.441406286379788e-05), math.log(0.05))), 2.441406286379788e-05, 0.05)
    skip_gain = jnp.clip(jax.random.uniform(own_keys[5], (CHANNELS,), jnp.float32, 0.25, 1.0), 0.25, 1.0)
    return {"query_gate": query_gate, "key_gate": key_gate, "value_input": value_input, "residues": residues, "decays": decays, "skip_gain": skip_gain}


def reference(query_gate, key_gate, value_input, residues, decays, skip_gain):
    signal = key_gate.astype(jnp.float32) * value_input.astype(jnp.float32)
    steps_time = jnp.arange(SEQ, dtype=jnp.float32)[:, None]
    kernel = jnp.zeros((SEQ, CHANNELS), jnp.float32)
    for mode_idx in range(MODES):
        kernel = kernel + residues[mode_idx] * jnp.sqrt(decays[mode_idx]) * jnp.exp(-decays[mode_idx] * steps_time)
    spec_signal = jnp.fft.rfft(signal, n=2 * SEQ, axis=0)
    spec_kernel = jnp.fft.rfft(kernel, n=2 * SEQ, axis=0)
    conv_out = jnp.fft.irfft(spec_signal * spec_kernel, n=2 * SEQ, axis=0)[:SEQ].astype(jnp.float32)
    return (query_gate.astype(jnp.float32) * (conv_out + skip_gain * signal)).astype(jnp.bfloat16)
```

```python
import functools

import jax
import jax.numpy as jnp
from jax import lax
from jax.experimental import pallas as pl
from jax.experimental.pallas import tpu as pltpu
from jax.sharding import PartitionSpec as P

SEG = 8
CHUNK = 8
LANES = 128
GROUPS = 1
BLOCK = 512


def row(ref, index, lanes):
    return jnp.broadcast_to(ref[pl.ds(index, 1), lanes], (SEG, LANES))


def gather_states(key_ref, value_ref, decays_ref, signal_ref, sums_ref, scan_ref, end_ref, natural, damp, damp_chunk):
    rows, width = key_ref.shape
    modes = decays_ref.shape[0]
    seg_len = rows // SEG
    chunks = seg_len // CHUNK
    segment = lax.broadcasted_iota(jnp.int32, (SEG, LANES), 0)

    @pl.loop(0, width // LANES)
    def _(block):
        lanes = pl.ds(pl.multiple_of(block * LANES, LANES), LANES)
        natural[...] = key_ref[:, lanes].astype(jnp.float32) * value_ref[:, lanes].astype(jnp.float32)
        decay = decays_ref[:, lanes]
        damp[...] = jnp.exp(-decay)
        damp_chunk[...] = jnp.exp(-CHUNK * decay)
        every = slice(None)

        def one_chunk(chunk, states):
            signal = [natural[pl.ds(chunk * CHUNK + step, SEG, stride=seg_len), :] for step in range(CHUNK)]
            for step in range(CHUNK):
                signal_ref[chunk * CHUNK + step, :, lanes] = signal[step]
            result = []
            for mode in range(modes):
                factor = row(damp, mode, every)
                total = signal[0]
                for step in range(1, CHUNK):
                    total = total * factor + signal[step]
                sums_ref[chunk, mode, :, lanes] = total
                result.append(states[mode] * row(damp_chunk, mode, every) + total)
            return result

        zeros = jnp.zeros((SEG, LANES), jnp.float32)
        states = lax.fori_loop(0, chunks, one_chunk, [zeros] * modes)
        for mode in range(modes):
            state = states[mode]
            decay_mode = row(decays_ref, mode, lanes)
            reach = 1
            while reach < SEG:
                factor = jnp.where(segment >= reach, jnp.exp(-(reach * seg_len) * decay_mode), 0.0)
                state = state + factor * pltpu.roll(state, reach, 0)
                reach *= 2
            scan_ref[mode, :, lanes] = state
            end_ref[pl.ds(mode, 1), lanes] = state[SEG - 1 :, :]


def near_terms(signal_ref, residues_ref, decays_ref, skip_ref, near_ref):
    steps, _, width = signal_ref.shape
    chunks = steps // CHUNK

    @pl.loop(0, width // LANES)
    def _(block):
        lanes = pl.ds(pl.multiple_of(block * LANES, LANES), LANES)
        decay = decays_ref[:, lanes]
        term = residues_ref[:, lanes] * jnp.sqrt(decay)
        damp = jnp.exp(-decay)
        taps = []
        for step in range(CHUNK):
            tap = jnp.sum(term, 0, keepdims=True)
            if step == 0:
                tap = tap + skip_ref[:, lanes]
            taps.append(jnp.broadcast_to(tap, (SEG, LANES)))
            term = term * damp

        @pl.loop(0, chunks)
        def _(chunk):
            signal = [signal_ref[chunk * CHUNK + step, :, lanes] for step in range(CHUNK)]
            for step in range(CHUNK):
                total = taps[0] * signal[step]
                for back in range(1, step + 1):
                    total = total + taps[back] * signal[step - back]
                near_ref[chunk * CHUNK + step, :, lanes] = total


def spread_states(query_ref, near_ref, sums_ref, scan_ref, enter_ref, residues_ref, decays_ref, mixed_ref, natural, damp, weight):
    rows, width = query_ref.shape
    modes = decays_ref.shape[0]
    seg_len = rows // SEG
    chunks = seg_len // CHUNK
    segment = lax.broadcasted_iota(jnp.int32, (SEG, LANES), 0)
    passed = (segment * seg_len).astype(jnp.float32)

    @pl.loop(0, width // LANES)
    def _(block):
        lanes = pl.ds(pl.multiple_of(block * LANES, LANES), LANES)
        decay = decays_ref[:, lanes]
        damp[...] = jnp.exp(-decay)
        weight[...] = residues_ref[:, lanes] * jnp.sqrt(decay) * damp[...]
        every = slice(None)
        states = []
        for mode in range(modes):
            before = jnp.where(segment >= 1, pltpu.roll(scan_ref[mode, :, lanes], 1, 0), 0.0)
            state = before + jnp.exp(-passed * row(decays_ref, mode, lanes)) * row(enter_ref, mode, lanes)
            states.append(state * row(weight, mode, every))

        def one_chunk(chunk, states):
            conv = [near_ref[chunk * CHUNK + step, :, lanes] for step in range(CHUNK)]
            result = []
            for mode in range(modes):
                factor = row(damp, mode, every)
                state = states[mode]
                for step in range(CHUNK):
                    conv[step] = conv[step] + state
                    state = state * factor
                result.append(state + row(weight, mode, every) * sums_ref[chunk, mode, :, lanes])
            for step in range(CHUNK):
                natural[pl.ds(chunk * CHUNK + step, SEG, stride=seg_len), :] = conv[step]
            return result

        lax.fori_loop(0, chunks, one_chunk, states)
        mixed_ref[:, lanes] = (query_ref[:, lanes].astype(jnp.float32) * natural[...]).astype(jnp.bfloat16)


def shards(query_gate, key_gate, value_input, residues, decays, skip_gain):
    rows, width = key_gate.shape
    modes = residues.shape[0]
    seg_len = rows // SEG
    chunks = seg_len // CHUNK
    ctx_size = lax.axis_size("ctx")
    ctx_rank = lax.axis_index("ctx")
    skip_gain = skip_gain[None, :]
    group = width // GROUPS
    block = min(BLOCK, group)
    blocks = group // block
    real = functools.partial(jax.ShapeDtypeStruct, dtype=jnp.float32)
    scratch = [pltpu.VMEM((rows, LANES), jnp.float32)] + [pltpu.VMEM((modes, LANES), jnp.float32)] * 2
    params = pltpu.CompilerParams(vmem_limit_bytes=48 * 2**20)
    points = rows * group

    def flat(count, part=0):
        return pl.BlockSpec((count, block), lambda i: (0, part * blocks + i))

    def deep(*lead):
        return pl.BlockSpec(lead + (block,), lambda i: (0,) * len(lead) + (i,))

    first, mixed = [], []
    for part in range(GROUPS):
        first.append(
            pl.pallas_call(
                gather_states,
                grid=(blocks,),
                in_specs=[flat(rows, part), flat(rows, part), flat(modes, part)],
                out_specs=[deep(seg_len, SEG), deep(chunks, modes, SEG), deep(modes, SEG), flat(modes)],
                out_shape=[
                    real((seg_len, SEG, group)),
                    real((chunks, modes, SEG, group)),
                    real((modes, SEG, group)),
                    real((modes, group)),
                ],
                scratch_shapes=scratch,
                compiler_params=params,
                cost_estimate=pl.CostEstimate(flops=2 * modes * points, bytes_accessed=8 * points, transcendentals=0),
                name="gather_states",
            )(key_gate, value_input, decays)
        )
    enters = []
    for part in range(GROUPS):
        decay = decays[:, part * group : (part + 1) * group]
        total = first[part][3]
        enter = jnp.zeros_like(total)
        reach = 1
        while reach < ctx_size:
            come = lax.ppermute(total, "ctx", [(i, i ^ reach) for i in range(ctx_size)])
            upper = (ctx_rank // reach) % 2 == 1
            behind = (ctx_rank % reach * rows).astype(jnp.float32)
            enter = enter + jnp.where(upper, jnp.exp(-behind * decay) * come, 0.0)
            over = jnp.exp(-float(reach * rows) * decay)
            total = jnp.where(upper, total + over * come, come + over * total)
            reach *= 2
        enters.append(enter)
    for part in range(GROUPS):
        signal, sums, scan, _ = first[part]
        near = pl.pallas_call(
            near_terms,
            grid=(blocks,),
            in_specs=[deep(seg_len, SEG), flat(modes, part), flat(modes, part), flat(1, part)],
            out_specs=deep(seg_len, SEG),
            out_shape=real((seg_len, SEG, group)),
            compiler_params=params,
            cost_estimate=pl.CostEstimate(flops=9 * points, bytes_accessed=8 * points, transcendentals=0),
            name="near_terms",
        )(signal, residues, decays, skip_gain)
        mixed.append(
            pl.pallas_call(
                spread_states,
                grid=(blocks,),
                in_specs=[
                    flat(rows, part),
                    deep(seg_len, SEG),
                    deep(chunks, modes, SEG),
                    deep(modes, SEG),
                    flat(modes),
                    flat(modes, part),
                    flat(modes, part),
                ],
                out_specs=flat(rows),
                out_shape=jax.ShapeDtypeStruct((rows, group), jnp.bfloat16),
                scratch_shapes=scratch,
                compiler_params=params,
                cost_estimate=pl.CostEstimate(flops=2 * modes * points, bytes_accessed=12 * points, transcendentals=0),
                name="spread_states",
            )(query_gate, near, sums, scan, enters[part], residues, decays)
        )
    return jnp.concatenate(mixed, 1)


def solution(mesh):
    placed = (
        P("ctx", "chan"),
        P("ctx", "chan"),
        P("ctx", "chan"),
        P(None, "chan"),
        P(None, "chan"),
        P("chan"),
    )
    return jax.shard_map(shards, mesh=mesh, in_specs=placed, out_specs=P("ctx", "chan"), check_vma=False)
```

```python
import functools

import jax
import jax.numpy as jnp
from jax import lax
from jax.experimental import pallas as pl
from jax.experimental.pallas import tpu as pltpu
from jax.sharding import PartitionSpec as P

SEG = 8
CHUNK = 8
LANES = 128
GROUPS = 2
SLABS = (0, 1, 4)
MIB = 2**20

VMEM = pl.BlockSpec(memory_space=pltpu.VMEM)
HBM = pl.BlockSpec(memory_space=pltpu.HBM)


def row(ref, index, lanes=slice(None)):
    return jnp.broadcast_to(ref[pl.ds(index, 1), lanes], (SEG, LANES))


def lane_block(block):
    return pl.ds(pl.multiple_of(block * LANES, LANES), LANES)


def gather_states(
    first, key_ref, value_ref, decays_ref, signal_ref, sums_ref, scan_ref, end_ref, keys, values, rates, natural, turned, damp, damp_chunk, sems
):
    rows, width = keys.shape
    modes = rates.shape[0]
    blocks = width // LANES
    seg_len = rows // SEG
    chunks = seg_len // CHUNK
    pitch = seg_len + 1

    rate_copy = pltpu.make_async_copy(decays_ref.at[:, pl.ds(first, width)], rates, sems.at[2, 0])
    starts = [start for start in SLABS if start < blocks]
    slabs = []
    for index, (start, stop) in enumerate(zip(starts, starts[1:] + [blocks])):
        inner = pl.ds(start * LANES, (stop - start) * LANES)
        outer = pl.ds(first + start * LANES, (stop - start) * LANES)
        slabs.append(
            (
                pltpu.make_async_copy(key_ref.at[:, outer], keys.at[:, inner], sems.at[0, index]),
                pltpu.make_async_copy(value_ref.at[:, outer], values.at[:, inner], sems.at[1, index]),
            )
        )
        for copy in slabs[-1]:
            copy.start()
        if index == 0:
            rate_copy.start()
    rate_copy.wait()

    @pl.loop(0, blocks)
    def _(block):
        lanes = lane_block(block)
        decay = rates[:, lanes]
        damp[...] = jnp.exp(-decay)
        damp_chunk[...] = jnp.exp(-CHUNK * decay)
        damp_segment = jnp.exp(-seg_len * decay)
        for start, copies in zip(starts, slabs):

            @pl.when(block == start)
            def _(copies=copies):
                for copy in copies:
                    copy.wait()

        for start in range(0, rows, 16):
            part = pl.ds(start, 16)
            place = start // seg_len * pitch + start % seg_len
            natural[pl.ds(place, 16), :] = keys[part, lanes].astype(jnp.float32) * values[part, lanes].astype(jnp.float32)
        states = [None] * modes
        for chunk in range(chunks):
            signal = [natural[pl.ds(chunk * CHUNK + step, SEG, stride=pitch), :] for step in range(CHUNK)]
            for step in range(CHUNK):
                signal_ref[chunk * CHUNK + step, :, lanes] = signal[step]
            for mode in range(modes):
                factor = row(damp, mode)
                total = signal[0]
                for step in range(1, CHUNK):
                    total = total * factor + signal[step]
                if chunk < chunks - 1:
                    sums_ref[chunk, mode, :, lanes] = total
                states[mode] = total if chunk == 0 else states[mode] * row(damp_chunk, mode) + total
        for mode in range(modes):
            turned[pl.ds(mode * (SEG + 1), SEG), :] = states[mode]
        state = jnp.zeros((modes, LANES), jnp.float32)
        for segment in range(SEG):
            scan_ref[segment, :, lanes] = state
            state = state * damp_segment + turned[pl.ds(segment, modes, stride=SEG + 1), :]
        end_ref[:, lanes] = state


def carry(first, positions, reach, opening, final, rank_ref, decays_ref, come_ref, *refs):
    decay = decays_ref[:, pl.ds(first, come_ref.shape[1])]
    come = come_ref[...]
    rank = rank_ref[0]
    upper = rank & reach != 0
    behind = ((rank & (reach - 1)) * (positions // reach)).astype(jnp.float32)
    refs = list(refs)
    total = None if final else refs.pop(0)[...]
    enter = 0.0 if opening else refs.pop(0)[...]
    refs[0][...] = enter + jnp.where(upper, jnp.exp(-behind * decay) * come, 0.0)
    if not final:
        over = jnp.exp(-positions * decay)
        refs[1][...] = jnp.where(upper, total + over * come, come + over * total)


def near_terms(first, signal_ref, residues_ref, decays_ref, skip_ref, near_ref):
    steps, _, width = signal_ref.shape
    chunks = steps // CHUNK

    @pl.loop(0, width // LANES)
    def _(block):
        lanes = lane_block(block)
        wide = pl.ds(pl.multiple_of(first + block * LANES, LANES), LANES)
        decay = decays_ref[:, wide]
        term = residues_ref[:, wide] * jnp.sqrt(decay)
        damp = jnp.exp(-decay)
        taps = []
        for step in range(CHUNK):
            tap = jnp.sum(term, 0, keepdims=True)
            if step == 0:
                tap = tap + skip_ref[:, wide]
            taps.append(jnp.broadcast_to(tap, (SEG, LANES)))
            term = term * damp
        for chunk in range(chunks):
            signal = [signal_ref[chunk * CHUNK + step, :, lanes] for step in range(CHUNK)]
            for step in range(CHUNK):
                total = taps[0] * signal[step]
                for back in range(1, step + 1):
                    total = total + taps[back] * signal[step - back]
                near_ref[chunk * CHUNK + step, :, lanes] = total


def spread_states(
    first, query_ref, near_ref, sums_ref, scan_ref, enter_ref, residues_ref, decays_ref, held_ref, mixed_ref, natural, turned, damp, weight, gated, sems
):
    rows = query_ref.shape[0]
    blocks = gated.shape[0]
    modes = decays_ref.shape[0]
    seg_len = rows // SEG
    chunks = seg_len // CHUNK
    pitch = seg_len + 1

    def copy(block):
        wide = pl.ds(pl.multiple_of(first + block * LANES, LANES), LANES)
        return pltpu.make_async_copy(gated.at[block], mixed_ref.at[:, wide], sems.at[block])

    @pl.loop(0, blocks)
    def _(block):
        lanes = lane_block(block)
        wide = pl.ds(pl.multiple_of(first + block * LANES, LANES), LANES)
        decay = decays_ref[:, wide]
        damp[...] = jnp.exp(-decay)
        scale = residues_ref[:, wide] * jnp.sqrt(decay) * jnp.exp(-decay)
        weight[...] = scale
        damp_segment = jnp.exp(-seg_len * decay)
        enter = enter_ref[:, lanes]
        for segment in range(SEG):
            turned[pl.ds(segment * (modes + 1), modes), :] = (scan_ref[segment, :, lanes] + enter) * scale
            enter = enter * damp_segment
        states = [turned[pl.ds(mode, SEG, stride=modes + 1), :] for mode in range(modes)]
        for chunk in range(chunks):
            conv = [near_ref[chunk * CHUNK + step, :, lanes] for step in range(CHUNK)]
            for mode in range(modes):
                factor = row(damp, mode)
                state = states[mode]
                for step in range(CHUNK):
                    conv[step] = conv[step] + state
                    if step < CHUNK - 1 or chunk < chunks - 1:
                        state = state * factor
                if chunk < chunks - 1:
                    states[mode] = state + row(weight, mode) * sums_ref[chunk, mode, :, lanes]
            for step in range(CHUNK):
                natural[pl.ds(chunk * CHUNK + step, SEG, stride=pitch), :] = conv[step]
        for start in range(0, rows, 16):
            part = pl.ds(start, 16)
            place = start // seg_len * pitch + start % seg_len
            gated[block, part, :] = (query_ref[part, wide].astype(jnp.float32) * natural[pl.ds(place, 16), :]).astype(jnp.bfloat16)
        copy(block).start()

    @pl.loop(0, blocks)
    def _(block):
        copy(block).wait()


def shards(query_gate, key_gate, value_input, residues, decays, skip_gain):
    rows, width = key_gate.shape
    modes = residues.shape[0]
    seg_len = rows // SEG
    chunks = seg_len // CHUNK
    ctx_size = lax.axis_size("ctx")
    ctx_rank = lax.axis_index("ctx")
    skip_gain = skip_gain[None, :]
    group = width // GROUPS
    blocks = group // LANES
    real = functools.partial(pltpu.VMEM, dtype=jnp.float32)
    natural = pltpu.VMEM((SEG * (seg_len + 1), LANES), jnp.float32)
    table = pltpu.VMEM((modes, LANES), jnp.float32)
    points = rows * group

    gathered = []
    for part in range(GROUPS):
        gathered.append(
            pl.pallas_call(
                functools.partial(gather_states, part * group),
                in_specs=[HBM, HBM, HBM],
                out_specs=[VMEM] * 4,
                out_shape=[
                    real((seg_len, SEG, group)),
                    real((chunks - 1, modes, SEG, group)),
                    real((SEG, modes, group)),
                    real((modes, group)),
                ],
                scratch_shapes=[
                    pltpu.VMEM((rows, group), jnp.bfloat16),
                    pltpu.VMEM((rows, group), jnp.bfloat16),
                    pltpu.VMEM((modes, group), jnp.float32),
                    natural,
                    pltpu.VMEM((modes * (SEG + 1), LANES), jnp.float32),
                    table,
                    table,
                    pltpu.SemaphoreType.DMA((3, len(SLABS))),
                ],
                compiler_params=pltpu.CompilerParams(vmem_limit_bytes=12 * MIB),
                cost_estimate=pl.CostEstimate(flops=2 * modes * points, bytes_accessed=4 * points, transcendentals=0),
                name="gather_states",
            )(*(pltpu.with_memory_space_constraint(array, pltpu.HBM) for array in (key_gate, value_input, decays)))
        )
    rank = ctx_rank.astype(jnp.int32).reshape(1)
    enters = []
    for part in range(GROUPS):
        total = gathered[part][3]
        enter = None
        reach = 1
        while reach < ctx_size:
            come = lax.ppermute(total, "ctx", [(i, i ^ reach) for i in range(ctx_size)])
            final = 2 * reach == ctx_size
            operands = [rank, decays, come] + ([] if final else [total]) + ([] if enter is None else [enter])
            result = pl.pallas_call(
                functools.partial(carry, part * group, reach * rows, reach, reach == 1, final),
                in_specs=[pl.BlockSpec(memory_space=pltpu.SMEM)] + [VMEM] * (len(operands) - 1),
                out_specs=[VMEM] * (1 if final else 2),
                out_shape=[real((modes, group))] * (1 if final else 2),
                compiler_params=pltpu.CompilerParams(vmem_limit_bytes=4 * MIB),
                name="carry",
            )(*operands)
            enter = result[0]
            total = result[-1]
            reach *= 2
        enters.append(enter)
    mixed = None
    for part in range(GROUPS):
        signal, sums, scan, _ = gathered[part]
        near = pl.pallas_call(
            functools.partial(near_terms, part * group),
            in_specs=[VMEM] * 4,
            out_specs=VMEM,
            out_shape=real((seg_len, SEG, group)),
            compiler_params=pltpu.CompilerParams(vmem_limit_bytes=12 * MIB),
            cost_estimate=pl.CostEstimate(flops=9 * points, bytes_accessed=0, transcendentals=0),
            name="near_terms",
        )(signal, residues, decays, skip_gain)
        operands = [query_gate, near, sums, scan, enters[part], residues, decays]
        specs = [VMEM] * 7
        aliases = {}
        body = functools.partial(spread_states, part * group)
        if part:
            operands.append(mixed)
            specs.append(HBM)
            aliases = {7: 0}
        else:
            body = functools.partial(lambda body, *refs: body(*refs[:7], None, *refs[7:]), body)
        mixed = pl.pallas_call(
            body,
            in_specs=specs,
            out_specs=HBM,
            out_shape=jax.ShapeDtypeStruct((rows, width), jnp.bfloat16),
            input_output_aliases=aliases,
            scratch_shapes=[
                natural,
                pltpu.VMEM((SEG * (modes + 1), LANES), jnp.float32),
                table,
                table,
                pltpu.VMEM((blocks, rows, LANES), jnp.bfloat16),
                pltpu.SemaphoreType.DMA((blocks,)),
            ],
            compiler_params=pltpu.CompilerParams(vmem_limit_bytes=12 * MIB),
            cost_estimate=pl.CostEstimate(flops=2 * modes * points, bytes_accessed=2 * points, transcendentals=0),
            name="spread_states",
        )(*operands)
    return mixed


def solution(mesh):
    placed = (
        P("ctx", "chan"),
        P("ctx", "chan"),
        P("ctx", "chan"),
        P(None, "chan"),
        P(None, "chan"),
        P("chan"),
    )
    return jax.shard_map(shards, mesh=mesh, in_specs=placed, out_specs=P("ctx", "chan"), check_vma=False)
```

```python
import functools

import jax
import jax.numpy as jnp
from jax import lax
from jax.experimental import pallas as pl
from jax.experimental.pallas import tpu as pltpu
from jax.sharding import PartitionSpec as P

SEG = 8
CHUNK = 8
LANES = 128
GROUPS = 2
SLABS = (0, 1, 4)
MIB = 2**20

VMEM = pl.BlockSpec(memory_space=pltpu.VMEM)
HBM = pl.BlockSpec(memory_space=pltpu.HBM)


def row(ref, index, lanes=slice(None)):
    return jnp.broadcast_to(ref[pl.ds(index, 1), lanes], (SEG, LANES))


def lane_block(block):
    return pl.ds(pl.multiple_of(block * LANES, LANES), LANES)


def gather_states(
    first, key_ref, value_ref, decays_ref, signal_ref, sums_ref, scan_ref, end_ref, keys, values, rates, natural, turned, damp, damp_chunk, sems
):
    rows, width = keys.shape
    modes = rates.shape[0]
    blocks = width // LANES
    seg_len = rows // SEG
    chunks = seg_len // CHUNK
    pitch = seg_len + 1

    rate_copy = pltpu.make_async_copy(decays_ref.at[:, pl.ds(first, width)], rates, sems.at[2, 0])
    starts = [start for start in SLABS if start < blocks]
    slabs = []
    for index, (start, stop) in enumerate(zip(starts, starts[1:] + [blocks])):
        inner = pl.ds(start * LANES, (stop - start) * LANES)
        outer = pl.ds(first + start * LANES, (stop - start) * LANES)
        slabs.append(
            (
                pltpu.make_async_copy(key_ref.at[:, outer], keys.at[:, inner], sems.at[0, index]),
                pltpu.make_async_copy(value_ref.at[:, outer], values.at[:, inner], sems.at[1, index]),
            )
        )
        for copy in slabs[-1]:
            copy.start()
        if index == 0:
            rate_copy.start()
    rate_copy.wait()

    @pl.loop(0, blocks)
    def _(block):
        lanes = lane_block(block)
        decay = rates[:, lanes]
        damp[...] = jnp.exp(-decay)
        damp_chunk[...] = jnp.exp(-CHUNK * decay)
        damp_segment = jnp.exp(-seg_len * decay)
        for start, copies in zip(starts, slabs):

            @pl.when(block == start)
            def _(copies=copies):
                for copy in copies:
                    copy.wait()

        for start in range(0, rows, 16):
            part = pl.ds(start, 16)
            place = start // seg_len * pitch + start % seg_len
            natural[pl.ds(place, 16), :] = keys[part, lanes].astype(jnp.float32) * values[part, lanes].astype(jnp.float32)
        states = [None] * modes
        for chunk in range(chunks):
            signal = [natural[pl.ds(chunk * CHUNK + step, SEG, stride=pitch), :] for step in range(CHUNK)]
            for step in range(CHUNK):
                signal_ref[chunk * CHUNK + step, :, lanes] = signal[step]
            for mode in range(modes):
                factor = row(damp, mode)
                total = signal[0]
                for step in range(1, CHUNK):
                    total = total * factor + signal[step]
                if chunk < chunks - 1:
                    sums_ref[chunk, mode, :, lanes] = total
                states[mode] = total if chunk == 0 else states[mode] * row(damp_chunk, mode) + total
        for mode in range(modes):
            turned[pl.ds(mode * (SEG + 1), SEG), :] = states[mode]
        state = jnp.zeros((modes, LANES), jnp.float32)
        for segment in range(SEG):
            scan_ref[segment, :, lanes] = state
            state = state * damp_segment + turned[pl.ds(segment, modes, stride=SEG + 1), :]
        end_ref[:, lanes] = state


def carry(first, positions, reach, opening, final, decays_ref, come_ref, *refs):
    decay = decays_ref[:, pl.ds(first, come_ref.shape[1])]
    come = come_ref[...]
    rank = lax.axis_index("ctx")
    upper = rank & reach != 0
    behind = ((rank & (reach - 1)) * (positions // reach)).astype(jnp.float32)
    refs = list(refs)
    total = None if final else refs.pop(0)[...]
    enter = 0.0 if opening else refs.pop(0)[...]
    refs[0][...] = enter + jnp.where(upper, jnp.exp(-behind * decay) * come, 0.0)
    if not final:
        over = jnp.exp(-positions * decay)
        refs[1][...] = jnp.where(upper, total + over * come, come + over * total)


def near_terms(first, signal_ref, residues_ref, decays_ref, skip_ref, near_ref):
    steps, _, width = signal_ref.shape
    chunks = steps // CHUNK

    @pl.loop(0, width // LANES)
    def _(block):
        lanes = lane_block(block)
        wide = pl.ds(pl.multiple_of(first + block * LANES, LANES), LANES)
        decay = decays_ref[:, wide]
        term = residues_ref[:, wide] * jnp.sqrt(decay)
        damp = jnp.exp(-decay)
        taps = []
        for step in range(CHUNK):
            tap = jnp.sum(term, 0, keepdims=True)
            if step == 0:
                tap = tap + skip_ref[:, wide]
            taps.append(jnp.broadcast_to(tap, (SEG, LANES)))
            term = term * damp
        for chunk in range(chunks):
            signal = [signal_ref[chunk * CHUNK + step, :, lanes] for step in range(CHUNK)]
            for step in range(CHUNK):
                total = taps[0] * signal[step]
                for back in range(1, step + 1):
                    total = total + taps[back] * signal[step - back]
                near_ref[chunk * CHUNK + step, :, lanes] = total


def spread_states(
    first, query_ref, near_ref, sums_ref, scan_ref, enter_ref, residues_ref, decays_ref, held_ref, mixed_ref, natural, turned, damp, weight, gated, sems
):
    rows = query_ref.shape[0]
    blocks = gated.shape[0]
    modes = decays_ref.shape[0]
    seg_len = rows // SEG
    chunks = seg_len // CHUNK
    pitch = seg_len + 1

    def copy(block):
        wide = pl.ds(pl.multiple_of(first + block * LANES, LANES), LANES)
        return pltpu.make_async_copy(gated.at[block], mixed_ref.at[:, wide], sems.at[block])

    @pl.loop(0, blocks)
    def _(block):
        lanes = lane_block(block)
        wide = pl.ds(pl.multiple_of(first + block * LANES, LANES), LANES)
        decay = decays_ref[:, wide]
        damp[...] = jnp.exp(-decay)
        scale = residues_ref[:, wide] * jnp.sqrt(decay) * jnp.exp(-decay)
        weight[...] = scale
        damp_segment = jnp.exp(-seg_len * decay)
        enter = enter_ref[:, lanes]
        for segment in range(SEG):
            turned[pl.ds(segment * (modes + 1), modes), :] = (scan_ref[segment, :, lanes] + enter) * scale
            enter = enter * damp_segment
        states = [turned[pl.ds(mode, SEG, stride=modes + 1), :] for mode in range(modes)]
        for chunk in range(chunks):
            conv = [near_ref[chunk * CHUNK + step, :, lanes] for step in range(CHUNK)]
            for mode in range(modes):
                factor = row(damp, mode)
                state = states[mode]
                for step in range(CHUNK):
                    conv[step] = conv[step] + state
                    if step < CHUNK - 1 or chunk < chunks - 1:
                        state = state * factor
                if chunk < chunks - 1:
                    states[mode] = state + row(weight, mode) * sums_ref[chunk, mode, :, lanes]
            for step in range(CHUNK):
                natural[pl.ds(chunk * CHUNK + step, SEG, stride=pitch), :] = conv[step]
        for start in range(0, rows, 16):
            part = pl.ds(start, 16)
            place = start // seg_len * pitch + start % seg_len
            gated[block, part, :] = (query_ref[part, wide].astype(jnp.float32) * natural[pl.ds(place, 16), :]).astype(jnp.bfloat16)
        copy(block).start()

    @pl.loop(0, blocks)
    def _(block):
        copy(block).wait()


def shards(query_gate, key_gate, value_input, residues, decays, skip_gain):
    rows, width = key_gate.shape
    modes = residues.shape[0]
    seg_len = rows // SEG
    chunks = seg_len // CHUNK
    ctx_size = lax.axis_size("ctx")
    skip_gain = skip_gain[None, :]
    group = width // GROUPS
    blocks = group // LANES
    real = functools.partial(pltpu.VMEM, dtype=jnp.float32)
    natural = pltpu.VMEM((SEG * (seg_len + 1), LANES), jnp.float32)
    table = pltpu.VMEM((modes, LANES), jnp.float32)
    points = rows * group

    gathered = []
    for part in range(GROUPS):
        gathered.append(
            pl.pallas_call(
                functools.partial(gather_states, part * group),
                in_specs=[HBM, HBM, HBM],
                out_specs=[VMEM] * 4,
                out_shape=[
                    real((seg_len, SEG, group)),
                    real((chunks - 1, modes, SEG, group)),
                    real((SEG, modes, group)),
                    real((modes, group)),
                ],
                scratch_shapes=[
                    pltpu.VMEM((rows, group), jnp.bfloat16),
                    pltpu.VMEM((rows, group), jnp.bfloat16),
                    pltpu.VMEM((modes, group), jnp.float32),
                    natural,
                    pltpu.VMEM((modes * (SEG + 1), LANES), jnp.float32),
                    table,
                    table,
                    pltpu.SemaphoreType.DMA((3, len(SLABS))),
                ],
                compiler_params=pltpu.CompilerParams(vmem_limit_bytes=12 * MIB),
                cost_estimate=pl.CostEstimate(flops=2 * modes * points, bytes_accessed=4 * points, transcendentals=0),
                name="gather_states",
            )(*(pltpu.with_memory_space_constraint(array, pltpu.HBM) for array in (key_gate, value_input, decays)))
        )
    enters = []
    for part in range(GROUPS):
        total = gathered[part][3]
        enter = None
        reach = 1
        while reach < ctx_size:
            come = lax.ppermute(total, "ctx", [(i, i ^ reach) for i in range(ctx_size)])
            final = 2 * reach == ctx_size
            operands = [decays, come] + ([] if final else [total]) + ([] if enter is None else [enter])
            result = pl.pallas_call(
                functools.partial(carry, part * group, reach * rows, reach, reach == 1, final),
                in_specs=[VMEM] * len(operands),
                out_specs=[VMEM] * (1 if final else 2),
                out_shape=[real((modes, group))] * (1 if final else 2),
                compiler_params=pltpu.CompilerParams(vmem_limit_bytes=4 * MIB),
                name="carry",
            )(*operands)
            enter = result[0]
            total = result[-1]
            reach *= 2
        enters.append(enter)
    mixed = None
    for part in range(GROUPS):
        signal, sums, scan, _ = gathered[part]
        near = pl.pallas_call(
            functools.partial(near_terms, part * group),
            in_specs=[VMEM] * 4,
            out_specs=VMEM,
            out_shape=real((seg_len, SEG, group)),
            compiler_params=pltpu.CompilerParams(vmem_limit_bytes=12 * MIB),
            cost_estimate=pl.CostEstimate(flops=9 * points, bytes_accessed=0, transcendentals=0),
            name="near_terms",
        )(signal, residues, decays, skip_gain)
        operands = [query_gate, near, sums, scan, enters[part], residues, decays]
        specs = [VMEM] * 7
        aliases = {}
        body = functools.partial(spread_states, part * group)
        if part:
            operands.append(mixed)
            specs.append(HBM)
            aliases = {7: 0}
        else:
            body = functools.partial(lambda body, *refs: body(*refs[:7], None, *refs[7:]), body)
        mixed = pl.pallas_call(
            body,
            in_specs=specs,
            out_specs=HBM,
            out_shape=jax.ShapeDtypeStruct((rows, width), jnp.bfloat16),
            input_output_aliases=aliases,
            scratch_shapes=[
                natural,
                pltpu.VMEM((SEG * (modes + 1), LANES), jnp.float32),
                table,
                table,
                pltpu.VMEM((blocks, rows, LANES), jnp.bfloat16),
                pltpu.SemaphoreType.DMA((blocks,)),
            ],
            compiler_params=pltpu.CompilerParams(vmem_limit_bytes=12 * MIB),
            cost_estimate=pl.CostEstimate(flops=2 * modes * points, bytes_accessed=2 * points, transcendentals=0),
            name="spread_states",
        )(*operands)
    return mixed


def solution(mesh):
    placed = (
        P("ctx", "chan"),
        P("ctx", "chan"),
        P("ctx", "chan"),
        P(None, "chan"),
        P(None, "chan"),
        P("chan"),
    )
    return jax.shard_map(shards, mesh=mesh, in_specs=placed, out_specs=P("ctx", "chan"), check_vma=False)
```

```python
import functools

import jax
import jax.numpy as jnp
from jax import lax
from jax.experimental import pallas as pl
from jax.experimental.pallas import tpu as pltpu
from jax.sharding import PartitionSpec as P

SEG = 8
CHUNK = 8
LANES = 128
LEAD = 9
SLABS = (0, 1, 4)
MIB = 2**20

VMEM = pl.BlockSpec(memory_space=pltpu.VMEM)
HBM = pl.BlockSpec(memory_space=pltpu.HBM)


def row(ref, index, lanes=slice(None)):
    return jnp.broadcast_to(ref[pl.ds(index, 1), lanes], (SEG, LANES))


def lane_block(block):
    return pl.ds(pl.multiple_of(block * LANES, LANES), LANES)


def gather_states(first, key_ref, value_ref, decays_ref, signal_ref, sums_ref, scan_ref, end_ref, natural, turned, damp, damp_chunk, arrive=None):
    rows, width = key_ref.shape
    modes = decays_ref.shape[0]
    seg_len = rows // SEG
    chunks = seg_len // CHUNK
    pitch = seg_len + 1

    @pl.loop(0, width // LANES)
    def _(block):
        if arrive is not None:
            arrive(block)
        lanes = lane_block(block)
        decay = decays_ref[:, pl.ds(pl.multiple_of(first + block * LANES, LANES), LANES)]
        damp[...] = jnp.exp(-decay)
        damp_chunk[...] = jnp.exp(-CHUNK * decay)
        damp_segment = jnp.exp(-seg_len * decay)
        for start in range(0, rows, 16):
            part = pl.ds(start, 16)
            place = start // seg_len * pitch + start % seg_len
            natural[pl.ds(place, 16), :] = key_ref[part, lanes].astype(jnp.float32) * value_ref[part, lanes].astype(jnp.float32)
        states = [None] * modes
        for chunk in range(chunks):
            signal = [natural[pl.ds(chunk * CHUNK + step, SEG, stride=pitch), :] for step in range(CHUNK)]
            for step in range(CHUNK):
                signal_ref[chunk * CHUNK + step, :, lanes] = signal[step]
            for mode in range(modes):
                factor = row(damp, mode)
                total = signal[0]
                for step in range(1, CHUNK):
                    total = total * factor + signal[step]
                if chunk < chunks - 1:
                    sums_ref[chunk, mode, :, lanes] = total
                states[mode] = total if chunk == 0 else states[mode] * row(damp_chunk, mode) + total
        for mode in range(modes):
            turned[pl.ds(mode * (SEG + 1), SEG), :] = states[mode]
        state = jnp.zeros((modes, LANES), jnp.float32)
        for segment in range(SEG):
            scan_ref[segment, :, lanes] = state
            state = state * damp_segment + turned[pl.ds(segment, modes, stride=SEG + 1), :]
        end_ref[:, lanes] = state


def load_and_gather(
    key_ref, value_ref, query_ref, decays_ref, signal_ref, sums_ref, scan_ref, end_ref, later_key_ref, later_value_ref, later_query_ref, natural, turned, damp, damp_chunk, keys, values, rates, sems
):
    width = keys.shape[1]
    blocks = width // LANES
    rate_copy = pltpu.make_async_copy(decays_ref.at[:, pl.ds(0, width)], rates, sems.at[2, 0])
    starts = [start for start in SLABS if start < blocks]
    slabs = []
    for index, (start, stop) in enumerate(zip(starts, starts[1:] + [blocks])):
        lanes = pl.ds(start * LANES, (stop - start) * LANES)
        slabs.append(
            (
                pltpu.make_async_copy(key_ref.at[:, lanes], keys.at[:, lanes], sems.at[0, index]),
                pltpu.make_async_copy(value_ref.at[:, lanes], values.at[:, lanes], sems.at[1, index]),
            )
        )
        for copy in slabs[-1]:
            copy.start()
        if index == 0:
            rate_copy.start()
    later = pl.ds(width, key_ref.shape[1] - width)
    later_copies = (
        pltpu.make_async_copy(key_ref.at[:, later], later_key_ref, sems.at[2, 1]),
        pltpu.make_async_copy(value_ref.at[:, later], later_value_ref, sems.at[2, 2]),
        pltpu.make_async_copy(query_ref, later_query_ref, sems.at[2, 3]),
    )
    for copy in later_copies:
        copy.start()
    rate_copy.wait()

    def arrive(block):
        for start, copies in zip(starts, slabs):

            @pl.when(block == start)
            def _(copies=copies):
                for copy in copies:
                    copy.wait()

    gather_states(0, keys, values, rates, signal_ref, sums_ref, scan_ref, end_ref, natural, turned, damp, damp_chunk, arrive)
    for copy in later_copies:
        copy.wait()


def carry(first, positions, reach, opening, final, after, decays_ref, come_ref, *refs):
    decay = decays_ref[:, pl.ds(first, come_ref.shape[1])]
    come = come_ref[...]
    rank = lax.axis_index("ctx")
    upper = rank & reach != 0
    behind = ((rank & (reach - 1)) * (positions // reach)).astype(jnp.float32)
    refs = list(refs[after:])
    total = None if final else refs.pop(0)[...]
    enter = 0.0 if opening else refs.pop(0)[...]
    refs[0][...] = enter + jnp.where(upper, jnp.exp(-behind * decay) * come, 0.0)
    if not final:
        over = jnp.exp(-positions * decay)
        refs[1][...] = jnp.where(upper, total + over * come, come + over * total)


def near_terms(first, signal_ref, sums_ref, residues_ref, decays_ref, skip_ref, near_ref, scaled_ref):
    steps, _, width = signal_ref.shape
    modes = decays_ref.shape[0]
    chunks = steps // CHUNK

    @pl.loop(0, width // LANES)
    def _(block):
        lanes = lane_block(block)
        wide = pl.ds(pl.multiple_of(first + block * LANES, LANES), LANES)
        decay = decays_ref[:, wide]
        term = residues_ref[:, wide] * jnp.sqrt(decay)
        damp = jnp.exp(-decay)
        weight = term * damp
        taps = []
        for step in range(CHUNK):
            tap = jnp.sum(term, 0, keepdims=True)
            if step == 0:
                tap = tap + skip_ref[:, wide]
            taps.append(jnp.broadcast_to(tap, (SEG, LANES)))
            term = term * damp
        for chunk in range(chunks):
            signal = [signal_ref[chunk * CHUNK + step, :, lanes] for step in range(CHUNK)]
            for step in range(CHUNK):
                total = taps[0] * signal[step]
                for back in range(1, step + 1):
                    total = total + taps[back] * signal[step - back]
                near_ref[chunk * CHUNK + step, :, lanes] = total
        for mode in range(modes):
            factor = jnp.broadcast_to(weight[mode : mode + 1, :], (SEG, LANES))
            scaled = [factor * sums_ref[chunk, mode, :, lanes] for chunk in range(chunks - 1)]
            for chunk in range(chunks - 1):
                scaled_ref[chunk, mode, :, lanes] = scaled[chunk]


def spread_states(first, query_ref, near_ref, sums_ref, scan_ref, enter_ref, residues_ref, decays_ref, gated_ref, natural, turned, damp, leave=None):
    rows, width = gated_ref.shape
    modes = decays_ref.shape[0]
    seg_len = rows // SEG
    chunks = seg_len // CHUNK
    pitch = seg_len + 1

    @pl.loop(0, width // LANES)
    def _(block):
        lanes = lane_block(block)
        wide = pl.ds(pl.multiple_of(first + block * LANES, LANES), LANES)
        decay = decays_ref[:, wide]
        once = jnp.exp(-decay)
        damp[...] = once
        scale = residues_ref[:, wide] * jnp.sqrt(decay) * once
        damp_segment = jnp.exp(-seg_len * decay)
        enter = enter_ref[:, lanes]
        for segment in range(SEG):
            turned[pl.ds(segment * (modes + 1), modes), :] = (scan_ref[segment, :, lanes] + enter) * scale
            enter = enter * damp_segment
        states = [turned[pl.ds(mode, SEG, stride=modes + 1), :] for mode in range(modes)]
        for chunk in range(chunks):
            conv = [near_ref[chunk * CHUNK + step, :, lanes] for step in range(CHUNK)]
            for mode in range(modes):
                factor = row(damp, mode)
                state = states[mode]
                for step in range(CHUNK):
                    conv[step] = conv[step] + state
                    if step < CHUNK - 1 or chunk < chunks - 1:
                        state = state * factor
                if chunk < chunks - 1:
                    states[mode] = state + sums_ref[chunk, mode, :, lanes]
            for step in range(CHUNK):
                natural[pl.ds(chunk * CHUNK + step, SEG, stride=pitch), :] = conv[step]
        for start in range(0, rows, 16):
            part = pl.ds(start, 16)
            place = start // seg_len * pitch + start % seg_len
            gated_ref[part, lanes] = (query_ref[part, wide].astype(jnp.float32) * natural[pl.ds(place, 16), :]).astype(jnp.bfloat16)
        if leave is not None:
            leave(block)


def spread_and_store(
    first, query_ref, near_ref, sums_ref, scan_ref, enter_ref, residues_ref, decays_ref, held_ref, mixed_ref, natural, turned, damp, gated, sems
):
    blocks = gated.shape[1] // LANES
    held_copy = pltpu.make_async_copy(held_ref, mixed_ref.at[:, pl.ds(0, first)], sems.at[blocks])
    held_copy.start()

    def copy(block):
        wide = pl.ds(pl.multiple_of(first + block * LANES, LANES), LANES)
        return pltpu.make_async_copy(gated.at[:, lane_block(block)], mixed_ref.at[:, wide], sems.at[block])

    spread_states(
        first, query_ref, near_ref, sums_ref, scan_ref, enter_ref, residues_ref, decays_ref, gated, natural, turned, damp, lambda block: copy(block).start()
    )

    @pl.loop(0, blocks)
    def _(block):
        copy(block).wait()

    held_copy.wait()


def shards(query_gate, key_gate, value_input, residues, decays, skip_gain):
    rows, width = key_gate.shape
    modes = residues.shape[0]
    seg_len = rows // SEG
    chunks = seg_len // CHUNK
    ctx_size = lax.axis_size("ctx")
    skip_gain = skip_gain[None, :]
    lead = width * LEAD // 16
    groups = [(0, lead), (lead, width - lead)]
    real = functools.partial(pltpu.VMEM, dtype=jnp.float32)
    half = functools.partial(pltpu.VMEM, dtype=jnp.bfloat16)
    natural = real((SEG * (seg_len + 1), LANES))
    table = real((modes, LANES))

    def cost(ops, moved, count):
        return pl.CostEstimate(flops=ops * rows * count, bytes_accessed=moved * rows * count, transcendentals=0)

    gathered = []
    for first, count in groups:
        shapes = [
            real((seg_len, SEG, count)),
            real((chunks - 1, modes, SEG, count)),
            real((SEG, modes, count)),
            real((modes, count)),
        ]
        scratch = [natural, real((modes * (SEG + 1), LANES)), table, table]
        if first == 0:
            later = half((rows, width - count))
            *states, later_keys, later_values, queries = pl.pallas_call(
                load_and_gather,
                in_specs=[HBM] * 4,
                out_specs=[VMEM] * 7,
                out_shape=shapes + [later, later, half((rows, width))],
                scratch_shapes=scratch
                + [half((rows, count)), half((rows, count)), real((modes, count)), pltpu.SemaphoreType.DMA((3, 4))],
                compiler_params=pltpu.CompilerParams(vmem_limit_bytes=12 * MIB),
                cost_estimate=cost(2 * modes, 19, count),
                name="load_and_gather",
            )(*(pltpu.with_memory_space_constraint(array, pltpu.HBM) for array in (key_gate, value_input, query_gate, decays)))
        else:
            states = pl.pallas_call(
                functools.partial(gather_states, first),
                in_specs=[VMEM] * 3,
                out_specs=[VMEM] * 4,
                out_shape=shapes,
                scratch_shapes=scratch,
                compiler_params=pltpu.CompilerParams(vmem_limit_bytes=4 * MIB),
                cost_estimate=cost(2 * modes, 19, count),
                name="gather_states",
            )(later_keys, later_values, decays)
        gathered.append(states)

    nears = []
    for (first, count), (signal, sums, _, _) in zip(groups, gathered):
        nears.append(
            pl.pallas_call(
                functools.partial(near_terms, first),
                in_specs=[VMEM] * 5,
                out_specs=[VMEM] * 2,
                out_shape=[real(signal.shape), real(sums.shape)],
                compiler_params=pltpu.CompilerParams(vmem_limit_bytes=4 * MIB),
                cost_estimate=cost(10, 7, count),
                name="near_terms",
            )(signal, sums, residues, decays, skip_gain)
        )

    held = None
    for part, (first, count) in enumerate(groups):
        total = gathered[part][3]
        enter = None
        reach = 1
        while reach < ctx_size:
            come = lax.ppermute(total, "ctx", [(i, i ^ reach) for i in range(ctx_size)])
            final = 2 * reach == ctx_size
            after = []
            if part and reach == 1:
                after = [near for near, _ in nears]
            elif part and final:
                after = [held]
            operands = [decays, come] + after + ([] if final else [total]) + ([] if enter is None else [enter])
            result = pl.pallas_call(
                functools.partial(carry, first, reach * rows, reach, reach == 1, final, len(after)),
                in_specs=[VMEM] * len(operands),
                out_specs=[VMEM] * (1 if final else 2),
                out_shape=[real((modes, count))] * (1 if final else 2),
                compiler_params=pltpu.CompilerParams(vmem_limit_bytes=4 * MIB),
                name="carry",
            )(*operands)
            enter = result[0]
            total = result[-1]
            reach *= 2
        operands = [queries, *nears[part], gathered[part][2], enter, residues, decays]
        scratch = [natural, real((SEG * (modes + 1), LANES)), table]
        if part == 0:
            held = pl.pallas_call(
                functools.partial(spread_states, first),
                in_specs=[VMEM] * len(operands),
                out_specs=VMEM,
                out_shape=half((rows, count)),
                scratch_shapes=scratch,
                compiler_params=pltpu.CompilerParams(vmem_limit_bytes=4 * MIB),
                cost_estimate=cost(2 * modes, 21, count),
                name="spread_states",
            )(*operands)
        else:
            mixed = pl.pallas_call(
                functools.partial(spread_and_store, first),
                in_specs=[VMEM] * (len(operands) + 1),
                out_specs=HBM,
                out_shape=jax.ShapeDtypeStruct((rows, width), jnp.bfloat16),
                scratch_shapes=scratch + [half((rows, count)), pltpu.SemaphoreType.DMA((count // LANES + 1,))],
                compiler_params=pltpu.CompilerParams(vmem_limit_bytes=6 * MIB),
                cost_estimate=cost(2 * modes, 21, count),
                name="spread_and_store",
            )(*operands, held)
    return mixed


def solution(mesh):
    placed = (
        P("ctx", "chan"),
        P("ctx", "chan"),
        P("ctx", "chan"),
        P(None, "chan"),
        P(None, "chan"),
        P("chan"),
    )
    return jax.shard_map(shards, mesh=mesh, in_specs=placed, out_specs=P("ctx", "chan"), check_vma=False)
```

```python
import functools

import jax
import jax.numpy as jnp
from jax import lax
from jax.experimental import pallas as pl
from jax.experimental.pallas import tpu as pltpu
from jax.sharding import PartitionSpec as P

SEG = 8
CHUNK = 8
LANES = 128
SLABS = (0, 1, 4)
MIB = 2**20

VMEM = pl.BlockSpec(memory_space=pltpu.VMEM)
HBM = pl.BlockSpec(memory_space=pltpu.HBM)


def row(ref, index, lanes=slice(None)):
    return jnp.broadcast_to(ref[pl.ds(index, 1), lanes], (SEG, LANES))


def lane_block(block):
    return pl.ds(pl.multiple_of(block * LANES, LANES), LANES)


def channels_of(other, count):
    mine = lax.axis_index("half")
    return pl.multiple_of((1 - mine if other else mine) * count, LANES)


def gather_states(other, key_ref, value_ref, decays_ref, signal_ref, sums_ref, scan_ref, natural, turned, damp, damp_chunk, end_ref=None, arrive=None):
    rows = key_ref.shape[0]
    blocks, _, modes, _ = scan_ref.shape
    seg_len = rows // SEG
    chunks = seg_len // CHUNK
    pitch = seg_len + 1
    first = channels_of(other, blocks * LANES) if other else 0

    @pl.loop(0, blocks)
    def _(block):
        if arrive is not None:
            arrive(block)
        lanes = lane_block(block)
        decay = decays_ref[:, pl.ds(pl.multiple_of(first + block * LANES, LANES), LANES)]
        damp[...] = jnp.exp(-decay)
        damp_chunk[...] = jnp.exp(-CHUNK * decay)
        damp_segment = jnp.exp(-seg_len * decay)
        for start in range(0, rows, 16):
            part = pl.ds(start, 16)
            place = start // seg_len * pitch + start % seg_len
            natural[pl.ds(place, 16), :] = key_ref[part, lanes].astype(jnp.float32) * value_ref[part, lanes].astype(jnp.float32)
        states = [None] * modes
        for chunk in range(chunks):
            signal = [natural[pl.ds(chunk * CHUNK + step, SEG, stride=pitch), :] for step in range(CHUNK)]
            for step in range(CHUNK):
                signal_ref[block, chunk * CHUNK + step] = signal[step]
            for mode in range(modes):
                factor = row(damp, mode)
                total = signal[0]
                for step in range(1, CHUNK):
                    total = total * factor + signal[step]
                if chunk < chunks - 1:
                    sums_ref[block, chunk, mode] = total
                states[mode] = total if chunk == 0 else states[mode] * row(damp_chunk, mode) + total
        for mode in range(modes):
            turned[pl.ds(mode * (SEG + 1), SEG), :] = states[mode]
        state = jnp.zeros((modes, LANES), jnp.float32)
        for segment in range(SEG):
            scan_ref[block, segment] = state
            if end_ref is not None or segment < SEG - 1:
                state = state * damp_segment + turned[pl.ds(segment, modes, stride=SEG + 1), :]
        if end_ref is not None:
            end_ref[:, lanes] = state


def load_and_gather(
    key_ref, value_ref, query_ref, decays_ref, signal_ref, sums_ref, scan_ref, end_ref, later_key_ref, later_value_ref, later_query_ref, natural, turned, damp, damp_chunk, keys, values, rates, sems
):
    blocks = scan_ref.shape[0]
    width = blocks * LANES
    first = channels_of(False, width)
    rate_copy = pltpu.make_async_copy(decays_ref.at[:, pl.ds(first, width)], rates, sems.at[2, 0])
    starts = [start for start in SLABS if start < blocks]
    slabs = []
    for index, (start, stop) in enumerate(zip(starts, starts[1:] + [blocks])):
        lanes = pl.ds(start * LANES, (stop - start) * LANES)
        wide = pl.ds(pl.multiple_of(first + start * LANES, LANES), (stop - start) * LANES)
        slabs.append(
            (
                pltpu.make_async_copy(key_ref.at[:, wide], keys.at[:, lanes], sems.at[0, index]),
                pltpu.make_async_copy(value_ref.at[:, wide], values.at[:, lanes], sems.at[1, index]),
            )
        )
        for copy in slabs[-1]:
            copy.start()
        if index == 0:
            rate_copy.start()
    later = pl.ds(channels_of(True, width), width)
    later_copies = (
        pltpu.make_async_copy(key_ref.at[:, later], later_key_ref.at[:, pl.ds(0, width)], sems.at[2, 1]),
        pltpu.make_async_copy(value_ref.at[:, later], later_value_ref.at[:, pl.ds(0, width)], sems.at[2, 2]),
        pltpu.make_async_copy(query_ref, later_query_ref.at[:, pl.ds(0, query_ref.shape[1])], sems.at[2, 3]),
    )
    for copy in later_copies:
        copy.start()
    rate_copy.wait()

    def arrive(block):
        for start, copies in zip(starts, slabs):

            @pl.when(block == start)
            def _(copies=copies):
                for copy in copies:
                    copy.wait()

    gather_states(False, keys, values, rates, signal_ref, sums_ref, scan_ref, natural, turned, damp, damp_chunk, end_ref, arrive)
    for copy in later_copies:
        copy.wait()


def carry(other, reach, radix, rows, after, decays_ref, total_ref, *refs):
    refs = list(refs[after:])
    come = [total_ref[...]] + [refs.pop(0)[...] for _ in range(1, radix)][::-1]
    enter = refs.pop(0)[...] if reach > 1 else 0.0
    count = total_ref.shape[1]
    decay = decays_ref[:, pl.ds(channels_of(other, count), count)]
    rank = lax.axis_index("ctx")
    digit = rank // reach & (radix - 1)
    inside = rank & (reach - 1)
    total = 0.0
    for turn in range(radix):
        source = digit ^ turn
        if turn:
            behind = jnp.maximum(digit - 1 - source, 0) * reach + inside
            enter = enter + jnp.where(source < digit, jnp.exp(-(behind * rows).astype(jnp.float32) * decay) * come[turn], 0.0)
        if len(refs) > 1:
            total = total + jnp.exp(-((radix - 1 - source) * (reach * rows)).astype(jnp.float32) * decay) * come[turn]
    refs[0][...] = enter
    if len(refs) > 1:
        refs[1][...] = total


def near_terms(other, signal_ref, sums_ref, residues_ref, decays_ref, skip_ref, near_ref, scaled_ref):
    blocks, steps, _, _ = signal_ref.shape
    modes = decays_ref.shape[0]
    chunks = steps // CHUNK
    first = channels_of(other, blocks * LANES)

    @pl.loop(0, blocks)
    def _(block):
        wide = pl.ds(pl.multiple_of(first + block * LANES, LANES), LANES)
        decay = decays_ref[:, wide]
        term = residues_ref[:, wide] * jnp.sqrt(decay)
        damp = jnp.exp(-decay)
        weight = term * damp
        taps = []
        for step in range(CHUNK):
            tap = jnp.sum(term, 0, keepdims=True)
            if step == 0:
                tap = tap + skip_ref[:, wide]
            taps.append(jnp.broadcast_to(tap, (SEG, LANES)))
            term = term * damp
        for chunk in range(chunks):
            signal = [signal_ref[block, chunk * CHUNK + step] for step in range(CHUNK)]
            for step in range(CHUNK):
                total = taps[0] * signal[step]
                for back in range(1, step + 1):
                    total = total + taps[back] * signal[step - back]
                near_ref[block, chunk * CHUNK + step] = total
        for mode in range(modes):
            factor = jnp.broadcast_to(weight[mode : mode + 1, :], (SEG, LANES))
            scaled = [factor * sums_ref[block, chunk, mode] for chunk in range(chunks - 1)]
            for chunk in range(chunks - 1):
                scaled_ref[block, chunk, mode] = scaled[chunk]


def spread_states(other, query_ref, near_ref, sums_ref, scan_ref, enter_ref, residues_ref, decays_ref, _, gated_ref, natural, turned, damp, leave=None):
    rows = gated_ref.shape[0]
    blocks, _, modes, _ = scan_ref.shape
    first = channels_of(other, blocks * LANES)
    seg_len = rows // SEG
    chunks = seg_len // CHUNK
    pitch = seg_len + 1

    @pl.loop(0, blocks)
    def _(block):
        lanes = lane_block(block)
        wide = pl.ds(pl.multiple_of(first + block * LANES, LANES), LANES)
        decay = decays_ref[:, wide]
        once = jnp.exp(-decay)
        damp[...] = once
        scale = residues_ref[:, wide] * jnp.sqrt(decay) * once
        damp_segment = jnp.exp(-seg_len * decay)
        enter = enter_ref[:, lanes]
        for segment in range(SEG):
            turned[pl.ds(segment * (modes + 1), modes), :] = (scan_ref[block, segment] + enter) * scale
            enter = enter * damp_segment
        states = [turned[pl.ds(mode, SEG, stride=modes + 1), :] for mode in range(modes)]
        for chunk in range(chunks):
            conv = [near_ref[block, chunk * CHUNK + step] for step in range(CHUNK)]
            for mode in range(modes):
                factor = row(damp, mode)
                state = states[mode]
                for step in range(CHUNK):
                    conv[step] = conv[step] + state
                    if step < CHUNK - 1 or chunk < chunks - 1:
                        state = state * factor
                if chunk < chunks - 1:
                    states[mode] = state + sums_ref[block, chunk, mode]
            for step in range(CHUNK):
                natural[pl.ds(chunk * CHUNK + step, SEG, stride=pitch), :] = conv[step]
        for start in range(0, rows, 16):
            part = pl.ds(start, 16)
            place = start // seg_len * pitch + start % seg_len
            gated_ref[part, lanes] = (query_ref[part, wide].astype(jnp.float32) * natural[pl.ds(place, 16), :]).astype(jnp.bfloat16)
        if leave is not None:
            leave(block)


def spread_and_store(
    other, query_ref, near_ref, sums_ref, scan_ref, enter_ref, residues_ref, decays_ref, held_ref, mixed_ref, natural, turned, damp, gated, sems
):
    blocks = scan_ref.shape[0]
    width = blocks * LANES
    first = channels_of(other, width)
    held_copy = pltpu.make_async_copy(held_ref.at[:, pl.ds(0, width)], mixed_ref.at[:, pl.ds(channels_of(not other, width), width)], sems.at[blocks])
    held_copy.start()

    def copy(block):
        wide = pl.ds(pl.multiple_of(first + block * LANES, LANES), LANES)
        return pltpu.make_async_copy(gated.at[:, lane_block(block)], mixed_ref.at[:, wide], sems.at[block])

    spread_states(
        other, query_ref, near_ref, sums_ref, scan_ref, enter_ref, residues_ref, decays_ref, None, gated, natural, turned, damp, lambda block: copy(block).start()
    )

    @pl.loop(0, blocks)
    def _(block):
        copy(block).wait()

    held_copy.wait()


def shards(query_gate, key_gate, value_input, residues, decays, skip_gain):
    rows, width = key_gate.shape
    modes = residues.shape[0]
    seg_len = rows // SEG
    chunks = seg_len // CHUNK
    ctx_size = lax.axis_size("ctx")
    count = width // lax.axis_size("half")
    blocks = count // LANES
    padded = count + LANES * (1 - blocks % 2)
    skip_gain = skip_gain[None, :]
    real = functools.partial(pltpu.VMEM, dtype=jnp.float32)
    half = functools.partial(pltpu.VMEM, dtype=jnp.bfloat16)
    natural = real((SEG * (seg_len + 1), LANES))
    table = real((modes, LANES))

    def call(body, operands, out_shape, scratch, ops, moved, in_specs=None, out_specs=None, limit=4):
        return pl.pallas_call(
            body,
            in_specs=in_specs or [VMEM] * len(operands),
            out_specs=out_specs or jax.tree.map(lambda _: VMEM, out_shape),
            out_shape=out_shape,
            scratch_shapes=scratch,
            compiler_params=pltpu.CompilerParams(vmem_limit_bytes=limit * MIB),
            cost_estimate=pl.CostEstimate(flops=ops * rows * count, bytes_accessed=moved * rows * count, transcendentals=0),
            name=getattr(body, "func", body).__name__,
        )(*operands)

    state_shapes = [
        real((blocks, seg_len, SEG, LANES)),
        real((blocks, chunks - 1, modes, SEG, LANES)),
        real((blocks, SEG, modes, LANES)),
    ]
    scratch = [natural, real((modes * (SEG + 1), LANES)), table, table]
    *mine, later_keys, later_values, queries = call(
        load_and_gather,
        [pltpu.with_memory_space_constraint(array, pltpu.HBM) for array in (key_gate, value_input, query_gate, decays)],
        state_shapes + [real((modes, count)), half((rows, padded)), half((rows, padded)), half((rows, width + LANES))],
        scratch + [half((rows, padded)), half((rows, padded)), real((modes, count)), pltpu.SemaphoreType.DMA((3, 4))],
        2 * modes,
        19,
        in_specs=[HBM] * 4,
        limit=8,
    )
    theirs = call(functools.partial(gather_states, True), [later_keys, later_values, decays], state_shapes, scratch, 2 * modes, 19)
    nears = [
        call(
            functools.partial(near_terms, other),
            [signal, sums, residues, decays, skip_gain],
            [real(signal.shape), real(sums.shape)],
            [],
            10,
            7,
        )
        for other, (signal, sums, *_) in ((False, mine), (True, theirs))
    ]

    total, enter, reach = mine[3], None, 1
    while reach < ctx_size:
        radix = min(4, ctx_size // reach)
        come = [lax.ppermute(total, "ctx", [(i, i ^ (turn * reach)) for i in range(ctx_size)]) for turn in reversed(range(1, radix))]
        after = [near for near, _ in nears] if reach == 1 else []
        last = radix * reach == ctx_size
        result = call(
            functools.partial(carry, False, reach, radix, rows, len(after)),
            [decays, total, *after, *come] + ([] if enter is None else [enter]),
            [real((modes, count))] * (1 if last else 2),
            [],
            0,
            0,
        )
        enter, total = result[0], result[-1]
        reach *= radix
    enter_theirs = lax.ppermute(enter, "half", [(0, 1), (1, 0)])

    scratch = [natural, real((SEG * (modes + 1), LANES)), table]
    held = call(
        functools.partial(spread_states, False),
        [queries, *nears[0], mine[2], enter, residues, decays, nears[1][0]],
        half((rows, padded)),
        scratch,
        2 * modes,
        21,
    )
    return call(
        functools.partial(spread_and_store, True),
        [queries, *nears[1], theirs[2], enter_theirs, residues, decays, held],
        jax.ShapeDtypeStruct((rows, width), jnp.bfloat16),
        scratch + [half((rows, padded)), pltpu.SemaphoreType.DMA((blocks + 1,))],
        2 * modes,
        21,
        out_specs=HBM,
        limit=6,
    )


def solution(mesh):
    placed = (
        P("ctx", "chan"),
        P("ctx", "chan"),
        P("ctx", "chan"),
        P(None, "chan"),
        P(None, "chan"),
        P("chan"),
    )
    return jax.shard_map(shards, mesh=mesh, in_specs=placed, out_specs=P("ctx", "chan"), check_vma=False)
```

```python
import functools

import jax
import jax.numpy as jnp
from jax import lax
from jax.experimental import pallas as pl
from jax.experimental.pallas import tpu as pltpu
from jax.sharding import PartitionSpec as P

SEG = 8
CHUNK = 8
LANES = 128
SLABS = (0, 2, 4)
PAIR = 2
MIB = 2**20
TURNS = {2: (1,), 4: (2, 3, 1)}

VMEM = pl.BlockSpec(memory_space=pltpu.VMEM)
HBM = pl.BlockSpec(memory_space=pltpu.HBM)


def row(ref, index, lanes=slice(None)):
    return jnp.broadcast_to(ref[pl.ds(index, 1), lanes], (SEG, LANES))


def lane_block(block):
    return pl.ds(pl.multiple_of(block * LANES, LANES), LANES)


def channels_of(other, count):
    mine = lax.axis_index("half")
    return pl.multiple_of((1 - mine if other else mine) * count, LANES)


def gather_states(other, key_ref, value_ref, decays_ref, signal_ref, sums_ref, scan_ref, *scratch, end_ref=None, arrive=None):
    rows = key_ref.shape[0]
    blocks, _, modes, _ = scan_ref.shape
    seg_len = rows // SEG
    chunks = seg_len // CHUNK
    pitch = seg_len + 1
    first = channels_of(other, blocks * LANES) if other else 0

    def one(block, natural, turned, damp, damp_chunk):
        lanes = lane_block(block)
        decay = decays_ref[:, pl.ds(pl.multiple_of(first + block * LANES, LANES), LANES)]
        damp[...] = jnp.exp(-decay)
        damp_chunk[...] = jnp.exp(-CHUNK * decay)
        damp_segment = jnp.exp(-seg_len * decay)
        for start in range(0, rows, 16):
            part = pl.ds(start, 16)
            place = start // seg_len * pitch + start % seg_len
            natural[pl.ds(place, 16), :] = key_ref[part, lanes].astype(jnp.float32) * value_ref[part, lanes].astype(jnp.float32)
        states = [None] * modes
        for chunk in range(chunks):
            signal = [natural[pl.ds(chunk * CHUNK + step, SEG, stride=pitch), :] for step in range(CHUNK)]
            for step in range(CHUNK):
                signal_ref[block, chunk * CHUNK + step] = signal[step]
            for mode in range(modes):
                factor = row(damp, mode)
                total = signal[0]
                for step in range(1, CHUNK):
                    total = total * factor + signal[step]
                if chunk < chunks - 1:
                    sums_ref[block, chunk, mode] = total
                states[mode] = total if chunk == 0 else states[mode] * row(damp_chunk, mode) + total
        for mode in range(modes):
            turned[pl.ds(mode * (SEG + 1), SEG), :] = states[mode]
        state = jnp.zeros((modes, LANES), jnp.float32)
        for segment in range(SEG):
            scan_ref[block, segment] = state
            if end_ref is not None or segment < SEG - 1:
                state = state * damp_segment + turned[pl.ds(segment, modes, stride=SEG + 1), :]
        if end_ref is not None:
            end_ref[:, lanes] = state

    @pl.loop(0, blocks // PAIR)
    def _(pair):
        if arrive is not None:
            arrive(pair)
        for turn in range(PAIR):
            one(pair * PAIR + turn, *scratch[turn::PAIR])


def load_and_gather(
    key_ref, value_ref, query_ref, decays_ref, signal_ref, sums_ref, scan_ref, end_ref, later_key_ref, later_value_ref, later_query_ref, *scratch
):
    *scratch, keys, values, rates, sems = scratch
    blocks = scan_ref.shape[0]
    width = blocks * LANES
    first = channels_of(False, width)
    rate_copy = pltpu.make_async_copy(decays_ref.at[:, pl.ds(first, width)], rates, sems.at[2, 0])
    starts = [start for start in SLABS if start < blocks]
    slabs = []
    for index, (start, stop) in enumerate(zip(starts, starts[1:] + [blocks])):
        lanes = pl.ds(start * LANES, (stop - start) * LANES)
        wide = pl.ds(pl.multiple_of(first + start * LANES, LANES), (stop - start) * LANES)
        slabs.append(
            (
                pltpu.make_async_copy(key_ref.at[:, wide], keys.at[:, lanes], sems.at[0, index]),
                pltpu.make_async_copy(value_ref.at[:, wide], values.at[:, lanes], sems.at[1, index]),
            )
        )
        for copy in slabs[-1]:
            copy.start()
        if index == 0:
            rate_copy.start()
    later = pl.ds(channels_of(True, width), width)
    later_copies = (
        pltpu.make_async_copy(key_ref.at[:, later], later_key_ref.at[:, pl.ds(0, width)], sems.at[2, 1]),
        pltpu.make_async_copy(value_ref.at[:, later], later_value_ref.at[:, pl.ds(0, width)], sems.at[2, 2]),
        pltpu.make_async_copy(query_ref, later_query_ref.at[:, pl.ds(0, query_ref.shape[1])], sems.at[2, 3]),
    )
    for copy in later_copies:
        copy.start()
    rate_copy.wait()

    def arrive(pair):
        for start, copies in zip(starts, slabs):

            @pl.when(pair * PAIR == start)
            def _(copies=copies):
                for copy in copies:
                    copy.wait()

    gather_states(False, keys, values, rates, signal_ref, sums_ref, scan_ref, *scratch, end_ref=end_ref, arrive=arrive)
    for copy in later_copies:
        copy.wait()


def carry(other, reach, radix, rows, after, decays_ref, total_ref, *refs):
    refs = list(refs[after:])
    come = {turn: refs.pop(0)[...] for turn in TURNS[radix]}
    come[0] = total_ref[...]
    enter = refs.pop(0)[...] if reach > 1 else 0.0
    count = total_ref.shape[1]
    decay = decays_ref[:, pl.ds(channels_of(other, count), count)]
    rank = lax.axis_index("ctx")
    digit = rank // reach & (radix - 1)
    inside = rank & (reach - 1)
    total = 0.0
    for turn in range(radix):
        source = digit ^ turn
        if turn:
            behind = jnp.maximum(digit - 1 - source, 0) * reach + inside
            enter = enter + jnp.where(source < digit, jnp.exp(-(behind * rows).astype(jnp.float32) * decay) * come[turn], 0.0)
        if len(refs) > 1:
            total = total + jnp.exp(-((radix - 1 - source) * (reach * rows)).astype(jnp.float32) * decay) * come[turn]
    refs[0][...] = enter
    if len(refs) > 1:
        refs[1][...] = total


def near_terms(other, signal_ref, sums_ref, residues_ref, decays_ref, skip_ref, near_ref, scaled_ref):
    blocks, steps, _, _ = signal_ref.shape
    modes = decays_ref.shape[0]
    chunks = steps // CHUNK
    first = channels_of(other, blocks * LANES)

    @pl.loop(0, blocks)
    def _(block):
        wide = pl.ds(pl.multiple_of(first + block * LANES, LANES), LANES)
        decay = decays_ref[:, wide]
        term = residues_ref[:, wide] * jnp.sqrt(decay)
        damp = jnp.exp(-decay)
        weight = term * damp
        taps = []
        for step in range(CHUNK):
            tap = jnp.sum(term, 0, keepdims=True)
            if step == 0:
                tap = tap + skip_ref[:, wide]
            taps.append(jnp.broadcast_to(tap, (SEG, LANES)))
            term = term * damp
        for chunk in range(chunks):
            signal = [signal_ref[block, chunk * CHUNK + step] for step in range(CHUNK)]
            for step in range(CHUNK):
                total = taps[0] * signal[step]
                for back in range(1, step + 1):
                    total = total + taps[back] * signal[step - back]
                near_ref[block, chunk * CHUNK + step] = total
        for mode in range(modes):
            factor = jnp.broadcast_to(weight[mode : mode + 1, :], (SEG, LANES))
            scaled = [factor * sums_ref[block, chunk, mode] for chunk in range(chunks - 1)]
            for chunk in range(chunks - 1):
                scaled_ref[block, chunk, mode] = scaled[chunk]


def spread_states(other, query_ref, near_ref, sums_ref, scan_ref, enter_ref, residues_ref, decays_ref, _, gated_ref, *scratch, leave=None):
    rows = gated_ref.shape[0]
    blocks, _, modes, _ = scan_ref.shape
    first = channels_of(other, blocks * LANES)
    seg_len = rows // SEG
    chunks = seg_len // CHUNK
    pitch = seg_len + 1

    def one(block, natural, turned, damp):
        lanes = lane_block(block)
        wide = pl.ds(pl.multiple_of(first + block * LANES, LANES), LANES)
        decay = decays_ref[:, wide]
        once = jnp.exp(-decay)
        damp[...] = once
        scale = residues_ref[:, wide] * jnp.sqrt(decay) * once
        damp_segment = jnp.exp(-seg_len * decay)
        enter = enter_ref[:, lanes]
        for segment in range(SEG):
            turned[pl.ds(segment * (modes + 1), modes), :] = (scan_ref[block, segment] + enter) * scale
            enter = enter * damp_segment
        states = [turned[pl.ds(mode, SEG, stride=modes + 1), :] for mode in range(modes)]
        for chunk in range(chunks):
            conv = [near_ref[block, chunk * CHUNK + step] for step in range(CHUNK)]
            for mode in range(modes):
                factor = row(damp, mode)
                state = states[mode]
                for step in range(CHUNK):
                    conv[step] = conv[step] + state
                    if step < CHUNK - 1 or chunk < chunks - 1:
                        state = state * factor
                if chunk < chunks - 1:
                    states[mode] = state + sums_ref[block, chunk, mode]
            for step in range(CHUNK):
                natural[pl.ds(chunk * CHUNK + step, SEG, stride=pitch), :] = conv[step]
        for start in range(0, rows, 16):
            part = pl.ds(start, 16)
            place = start // seg_len * pitch + start % seg_len
            gated_ref[part, lanes] = (query_ref[part, wide].astype(jnp.float32) * natural[pl.ds(place, 16), :]).astype(jnp.bfloat16)

    @pl.loop(0, blocks // PAIR)
    def _(pair):
        for turn in range(PAIR):
            one(pair * PAIR + turn, *scratch[turn::PAIR])
        if leave is not None:
            for turn in range(PAIR):
                leave(pair * PAIR + turn)


def spread_and_store(
    other, query_ref, near_ref, sums_ref, scan_ref, enter_ref, residues_ref, decays_ref, held_ref, mixed_ref, *scratch
):
    *scratch, gated, sems = scratch
    blocks = scan_ref.shape[0]
    width = blocks * LANES
    first = channels_of(other, width)
    held_copy = pltpu.make_async_copy(held_ref.at[:, pl.ds(0, width)], mixed_ref.at[:, pl.ds(channels_of(not other, width), width)], sems.at[blocks])
    held_copy.start()

    def copy(block):
        wide = pl.ds(pl.multiple_of(first + block * LANES, LANES), LANES)
        return pltpu.make_async_copy(gated.at[:, lane_block(block)], mixed_ref.at[:, wide], sems.at[block])

    spread_states(
        other, query_ref, near_ref, sums_ref, scan_ref, enter_ref, residues_ref, decays_ref, None, gated, *scratch, leave=lambda block: copy(block).start()
    )

    @pl.loop(0, blocks)
    def _(block):
        copy(block).wait()

    held_copy.wait()


def shards(query_gate, key_gate, value_input, residues, decays, skip_gain):
    rows, width = key_gate.shape
    modes = residues.shape[0]
    seg_len = rows // SEG
    chunks = seg_len // CHUNK
    ctx_size = lax.axis_size("ctx")
    count = width // lax.axis_size("half")
    blocks = count // LANES
    padded = count + LANES * (1 - blocks % 2)
    skip_gain = skip_gain[None, :]
    real = functools.partial(pltpu.VMEM, dtype=jnp.float32)
    half = functools.partial(pltpu.VMEM, dtype=jnp.bfloat16)
    natural = real((SEG * (seg_len + 1), LANES))
    table = real((modes, LANES))

    def call(body, operands, out_shape, scratch, ops, moved, in_specs=None, out_specs=None, limit=4):
        return pl.pallas_call(
            body,
            in_specs=in_specs or [VMEM] * len(operands),
            out_specs=out_specs or jax.tree.map(lambda _: VMEM, out_shape),
            out_shape=out_shape,
            scratch_shapes=scratch,
            compiler_params=pltpu.CompilerParams(vmem_limit_bytes=limit * MIB),
            cost_estimate=pl.CostEstimate(flops=ops * rows * count, bytes_accessed=moved * rows * count, transcendentals=0),
            name=getattr(body, "func", body).__name__,
        )(*operands)

    state_shapes = [
        real((blocks, seg_len, SEG, LANES)),
        real((blocks, chunks - 1, modes, SEG, LANES)),
        real((blocks, SEG, modes, LANES)),
    ]
    scratch = [shape for shape in (natural, real((modes * (SEG + 1), LANES)), table, table) for _ in range(PAIR)]
    *mine, later_keys, later_values, queries = call(
        load_and_gather,
        [pltpu.with_memory_space_constraint(array, pltpu.HBM) for array in (key_gate, value_input, query_gate, decays)],
        state_shapes + [real((modes, count)), half((rows, padded)), half((rows, padded)), half((rows, width + LANES))],
        scratch + [half((rows, padded)), half((rows, padded)), real((modes, count)), pltpu.SemaphoreType.DMA((3, 4))],
        2 * modes,
        19,
        in_specs=[HBM] * 4,
        limit=8,
    )
    def near(other, states):
        signal, sums = states[:2]
        return call(
            functools.partial(near_terms, other),
            [signal, sums, residues, decays, skip_gain],
            [real(signal.shape), real(sums.shape)],
            [],
            10,
            7,
        )

    theirs = call(functools.partial(gather_states, True), [later_keys, later_values, decays], state_shapes, scratch, 2 * modes, 19)
    near_mine = near(False, mine)
    near_theirs = near(True, theirs)

    total, enter, reach = mine[3], None, 1
    while reach < ctx_size:
        radix = min(4, ctx_size // reach)
        come = [lax.ppermute(total, "ctx", [(i, i ^ (turn * reach)) for i in range(ctx_size)]) for turn in TURNS[radix]]
        after = [near_mine[0], near_theirs[0]] if reach == 1 else []
        last = radix * reach == ctx_size
        result = call(
            functools.partial(carry, False, reach, radix, rows, len(after)),
            [decays, total, *after, *come] + ([] if enter is None else [enter]),
            [real((modes, count))] * (1 if last else 2),
            [],
            0,
            0,
        )
        enter, total = result[0], result[-1]
        reach *= radix
    enter_theirs = lax.ppermute(enter, "half", [(0, 1), (1, 0)])

    scratch = [shape for shape in (natural, real((SEG * (modes + 1), LANES)), table) for _ in range(PAIR)]
    held = call(
        functools.partial(spread_states, False),
        [queries, *near_mine, mine[2], enter, residues, decays, near_theirs[0]],
        half((rows, padded)),
        scratch,
        2 * modes,
        21,
    )
    return call(
        functools.partial(spread_and_store, True),
        [queries, *near_theirs, theirs[2], enter_theirs, residues, decays, held],
        jax.ShapeDtypeStruct((rows, width), jnp.bfloat16),
        scratch + [half((rows, padded)), pltpu.SemaphoreType.DMA((blocks + 1,))],
        2 * modes,
        21,
        out_specs=HBM,
        limit=6,
    )


def solution(mesh):
    placed = (
        P("ctx", "chan"),
        P("ctx", "chan"),
        P("ctx", "chan"),
        P(None, "chan"),
        P(None, "chan"),
        P("chan"),
    )
    return jax.shard_map(shards, mesh=mesh, in_specs=placed, out_specs=P("ctx", "chan"), check_vma=False)
```

```python
import functools

import jax
import jax.numpy as jnp
from jax import lax
from jax.experimental import pallas as pl
from jax.experimental.pallas import tpu as pltpu
from jax.sharding import PartitionSpec as P

SEG = 8
CHUNK = 8
LANES = 128
SLABS = (0, 2, 4)
PAIR = 2
AHEAD = 2
MIB = 2**20
TURNS = {2: (1,), 4: (2, 3, 1)}

VMEM = pl.BlockSpec(memory_space=pltpu.VMEM)
HBM = pl.BlockSpec(memory_space=pltpu.HBM)


def leads():
    origin = True
    for axis in ("chan", "half", "ctx"):
        origin = (lax.axis_index(axis) == 0) & origin
    return origin


def row(ref, index, lanes=slice(None)):
    return jnp.broadcast_to(ref[pl.ds(index, 1), lanes], (SEG, LANES))


def lane_block(block):
    return pl.ds(pl.multiple_of(block * LANES, LANES), LANES)


def channels_of(other, count):
    mine = lax.axis_index("half")
    return pl.multiple_of((1 - mine if other else mine) * count, LANES)


def gather_states(other, key_ref, value_ref, decays_ref, signal_ref, sums_ref, scan_ref, *scratch, end_ref=None, arrive=None):
    rows = key_ref.shape[0]
    blocks, _, modes, _ = scan_ref.shape
    seg_len = rows // SEG
    chunks = seg_len // CHUNK
    pitch = seg_len + 1
    first = channels_of(other, blocks * LANES) if other else 0

    def one(block, natural, turned, damp, damp_chunk):
        lanes = lane_block(block)
        decay = decays_ref[:, pl.ds(pl.multiple_of(first + block * LANES, LANES), LANES)]
        damp[...] = jnp.exp(-decay)
        damp_chunk[...] = jnp.exp(-CHUNK * decay)
        damp_segment = jnp.exp(-seg_len * decay)
        for start in range(0, rows, 16):
            part = pl.ds(start, 16)
            place = start // seg_len * pitch + start % seg_len
            natural[pl.ds(place, 16), :] = key_ref[part, lanes].astype(jnp.float32) * value_ref[part, lanes].astype(jnp.float32)
        states = [None] * modes
        for chunk in range(chunks):
            signal = [natural[pl.ds(chunk * CHUNK + step, SEG, stride=pitch), :] for step in range(CHUNK)]
            for step in range(CHUNK):
                signal_ref[block, chunk * CHUNK + step] = signal[step]
            for mode in range(modes):
                factor = row(damp, mode)
                total = signal[0]
                for step in range(1, CHUNK):
                    total = total * factor + signal[step]
                if chunk < chunks - 1:
                    sums_ref[block, chunk, mode] = total
                states[mode] = total if chunk == 0 else states[mode] * row(damp_chunk, mode) + total
        for mode in range(modes):
            turned[pl.ds(mode * (SEG + 1), SEG), :] = states[mode]
        state = jnp.zeros((modes, LANES), jnp.float32)
        for segment in range(SEG):
            scan_ref[block, segment] = state
            if end_ref is not None or segment < SEG - 1:
                state = state * damp_segment + turned[pl.ds(segment, modes, stride=SEG + 1), :]
        if end_ref is not None:
            end_ref[:, lanes] = state

    @pl.loop(0, blocks // PAIR)
    def _(pair):
        if arrive is not None:
            arrive(pair)
        for turn in range(PAIR):
            one(pair * PAIR + turn, *scratch[turn::PAIR])


def load_and_gather(
    key_ref, value_ref, query_ref, decays_ref, signal_ref, sums_ref, scan_ref, end_ref, later_key_ref, later_value_ref, later_query_ref, *scratch
):
    *scratch, keys, values, rates, sems = scratch
    blocks = scan_ref.shape[0]
    width = blocks * LANES
    first = channels_of(False, width)
    rate_copy = pltpu.make_async_copy(decays_ref.at[:, pl.ds(first, width)], rates, sems.at[2, 0])
    starts = [start for start in SLABS if start < blocks]
    slabs = []
    for index, (start, stop) in enumerate(zip(starts, starts[1:] + [blocks])):
        lanes = pl.ds(start * LANES, (stop - start) * LANES)
        wide = pl.ds(pl.multiple_of(first + start * LANES, LANES), (stop - start) * LANES)
        slabs.append(
            (
                pltpu.make_async_copy(key_ref.at[:, wide], keys.at[:, lanes], sems.at[0, index]),
                pltpu.make_async_copy(value_ref.at[:, wide], values.at[:, lanes], sems.at[1, index]),
            )
        )
        for copy in slabs[-1]:
            copy.start()
        if index == 0:
            rate_copy.start()
    later = pl.ds(channels_of(True, width), width)
    later_copies = (
        pltpu.make_async_copy(key_ref.at[:, later], later_key_ref.at[:, pl.ds(0, width)], sems.at[2, 1]),
        pltpu.make_async_copy(value_ref.at[:, later], later_value_ref.at[:, pl.ds(0, width)], sems.at[2, 2]),
        pltpu.make_async_copy(query_ref, later_query_ref.at[:, pl.ds(0, query_ref.shape[1])], sems.at[2, 3]),
    )
    for copy in later_copies:
        copy.start()
    rate_copy.wait()

    def arrive(pair):
        for start, copies in zip(starts, slabs):

            @pl.when(pair * PAIR == start)
            def _(copies=copies):
                for copy in copies:
                    copy.wait()

    gather_states(False, keys, values, rates, signal_ref, sums_ref, scan_ref, *scratch, end_ref=end_ref, arrive=arrive)
    for copy in later_copies:
        copy.wait()


def carry(other, reach, radix, rows, after, decays_ref, total_ref, *refs):
    refs = list(refs[after:])
    come = {turn: refs.pop(0)[...] for turn in TURNS[radix]}
    come[0] = total_ref[...]
    enter = refs.pop(0)[...] if reach > 1 else 0.0
    count = total_ref.shape[1]
    decay = decays_ref[:, pl.ds(channels_of(other, count), count)]
    rank = lax.axis_index("ctx")
    digit = rank // reach & (radix - 1)
    inside = rank & (reach - 1)
    total = 0.0
    for turn in range(radix):
        source = digit ^ turn
        if turn:
            behind = jnp.maximum(digit - 1 - source, 0) * reach + inside
            enter = enter + jnp.where(source < digit, jnp.exp(-(behind * rows).astype(jnp.float32) * decay) * come[turn], 0.0)
        if len(refs) > 1:
            total = total + jnp.exp(-((radix - 1 - source) * (reach * rows)).astype(jnp.float32) * decay) * come[turn]
    refs[0][...] = enter
    if len(refs) > 1:
        refs[1][...] = total


def near_terms(other, share, signal_ref, sums_ref, residues_ref, decays_ref, skip_ref, *refs):
    near_ref, scaled_ref = refs[1:3] if share == "lead" else refs[-2:]
    blocks, steps, _, _ = signal_ref.shape
    modes = decays_ref.shape[0]
    chunks = steps // CHUNK
    first = channels_of(other, blocks * LANES)

    @pl.loop(0, blocks if share is None else jnp.where(leads() == (share == "lead"), blocks, 0))
    def _(block):
        wide = pl.ds(pl.multiple_of(first + block * LANES, LANES), LANES)
        decay = decays_ref[:, wide]
        term = residues_ref[:, wide] * jnp.sqrt(decay)
        damp = jnp.exp(-decay)
        weight = term * damp
        taps = []
        for step in range(CHUNK):
            tap = jnp.sum(term, 0, keepdims=True)
            if step == 0:
                tap = tap + skip_ref[:, wide]
            taps.append(jnp.broadcast_to(tap, (SEG, LANES)))
            term = term * damp
        for chunk in range(chunks):
            signal = [signal_ref[block, chunk * CHUNK + step] for step in range(CHUNK)]
            for step in range(CHUNK):
                total = taps[0] * signal[step]
                for back in range(1, step + 1):
                    total = total + taps[back] * signal[step - back]
                near_ref[block, chunk * CHUNK + step] = total
        for mode in range(modes):
            factor = jnp.broadcast_to(weight[mode : mode + 1, :], (SEG, LANES))
            scaled = [factor * sums_ref[block, chunk, mode] for chunk in range(chunks - 1)]
            for chunk in range(chunks - 1):
                scaled_ref[block, chunk, mode] = scaled[chunk]


def spread_states(other, span, enter_ref, query_ref, near_ref, sums_ref, scan_ref, residues_ref, decays_ref, gated_ref, *scratch, leave=None):
    rows = gated_ref.shape[0]
    blocks, _, modes, _ = scan_ref.shape
    first = channels_of(other, blocks * LANES)
    seg_len = rows // SEG
    chunks = seg_len // CHUNK
    pitch = seg_len + 1

    def one(block, natural, turned, damp):
        lanes = lane_block(block)
        wide = pl.ds(pl.multiple_of(first + block * LANES, LANES), LANES)
        decay = decays_ref[:, wide]
        once = jnp.exp(-decay)
        damp[...] = once
        scale = residues_ref[:, wide] * jnp.sqrt(decay) * once
        damp_segment = jnp.exp(-seg_len * decay)
        enter = jnp.zeros((modes, LANES), jnp.float32) if enter_ref is None else enter_ref[:, lanes]
        for segment in range(SEG):
            turned[pl.ds(segment * (modes + 1), modes), :] = (scan_ref[block, segment] + enter) * scale
            enter = enter * damp_segment
        states = [turned[pl.ds(mode, SEG, stride=modes + 1), :] for mode in range(modes)]
        for chunk in range(chunks):
            conv = [near_ref[block, chunk * CHUNK + step] for step in range(CHUNK)]
            for mode in range(modes):
                factor = row(damp, mode)
                state = states[mode]
                for step in range(CHUNK):
                    conv[step] = conv[step] + state
                    if step < CHUNK - 1 or chunk < chunks - 1:
                        state = state * factor
                if chunk < chunks - 1:
                    states[mode] = state + sums_ref[block, chunk, mode]
            for step in range(CHUNK):
                natural[pl.ds(chunk * CHUNK + step, SEG, stride=pitch), :] = conv[step]
        for start in range(0, rows, 16):
            part = pl.ds(start, 16)
            place = start // seg_len * pitch + start % seg_len
            gated_ref[part, lanes] = (query_ref[part, wide].astype(jnp.float32) * natural[pl.ds(place, 16), :]).astype(jnp.bfloat16)

    @pl.loop(*span)
    def _(pair):
        for turn in range(PAIR):
            one(pair * PAIR + turn, *scratch[turn::PAIR])
        if leave is not None:
            for turn in range(PAIR):
                leave(pair * PAIR + turn)


def spread_ahead(other, query_ref, near_ref, sums_ref, scan_ref, residues_ref, decays_ref, *refs):
    gated_ref, *scratch = refs[1:] if other else refs
    span = 0, jnp.where(leads(), AHEAD, 0)
    spread_states(other, span, None, query_ref, near_ref, sums_ref, scan_ref, residues_ref, decays_ref, gated_ref, *scratch)


def spread_mine(query_ref, near_ref, sums_ref, scan_ref, residues_ref, decays_ref, enter_ref, *refs):
    gated_ref, *scratch = refs[2:]
    span = jnp.where(leads(), AHEAD, 0), scan_ref.shape[0] // PAIR
    spread_states(False, span, enter_ref, query_ref, near_ref, sums_ref, scan_ref, residues_ref, decays_ref, gated_ref, *scratch)


def spread_and_store(
    query_ref, near_ref, sums_ref, scan_ref, residues_ref, decays_ref, enter_ref, held_ref, _, mixed_ref, gated, *scratch
):
    *scratch, sems = scratch
    blocks = scan_ref.shape[0]
    width = blocks * LANES
    first = channels_of(True, width)
    held_copy = pltpu.make_async_copy(held_ref.at[:, pl.ds(0, width)], mixed_ref.at[:, pl.ds(channels_of(False, width), width)], sems.at[blocks])
    held_copy.start()

    def copy(block):
        wide = pl.ds(pl.multiple_of(first + block * LANES, LANES), LANES)
        return pltpu.make_async_copy(gated.at[:, lane_block(block)], mixed_ref.at[:, wide], sems.at[block])

    ahead = jnp.where(leads(), AHEAD, 0)

    @pl.loop(0, ahead * PAIR)
    def _(block):
        copy(block).start()

    spread_states(
        True,
        (ahead, blocks // PAIR),
        enter_ref,
        query_ref,
        near_ref,
        sums_ref,
        scan_ref,
        residues_ref,
        decays_ref,
        gated,
        *scratch,
        leave=lambda block: copy(block).start(),
    )

    @pl.loop(0, blocks)
    def _(block):
        copy(block).wait()

    held_copy.wait()


def shards(query_gate, key_gate, value_input, residues, decays, skip_gain):
    rows, width = key_gate.shape
    modes = residues.shape[0]
    seg_len = rows // SEG
    chunks = seg_len // CHUNK
    ctx_size = lax.axis_size("ctx")
    count = width // lax.axis_size("half")
    blocks = count // LANES
    padded = count + LANES * (1 - blocks % 2)
    skip_gain = skip_gain[None, :]
    real = functools.partial(pltpu.VMEM, dtype=jnp.float32)
    half = functools.partial(pltpu.VMEM, dtype=jnp.bfloat16)
    natural = real((SEG * (seg_len + 1), LANES))
    table = real((modes, LANES))

    def call(body, operands, out_shape, scratch, ops, moved, in_specs=None, out_specs=None, limit=4, aliases=None):
        return pl.pallas_call(
            body,
            in_specs=in_specs or [VMEM] * len(operands),
            out_specs=out_specs or jax.tree.map(lambda _: VMEM, out_shape),
            out_shape=out_shape,
            scratch_shapes=scratch,
            input_output_aliases=aliases or {},
            compiler_params=pltpu.CompilerParams(vmem_limit_bytes=limit * MIB),
            cost_estimate=pl.CostEstimate(flops=ops * rows * count, bytes_accessed=moved * rows * count, transcendentals=0),
            name=getattr(body, "func", body).__name__,
        )(*operands)

    state_shapes = [
        real((blocks, seg_len, SEG, LANES)),
        real((blocks, chunks - 1, modes, SEG, LANES)),
        real((blocks, SEG, modes, LANES)),
    ]
    scratch = [shape for shape in (natural, real((modes * (SEG + 1), LANES)), table, table) for _ in range(PAIR)]
    *mine, later_keys, later_values, queries = call(
        load_and_gather,
        [pltpu.with_memory_space_constraint(array, pltpu.HBM) for array in (key_gate, value_input, query_gate, decays)],
        state_shapes + [real((modes, count)), half((rows, padded)), half((rows, padded)), half((rows, width + LANES))],
        scratch + [half((rows, padded)), half((rows, padded)), real((modes, count)), pltpu.SemaphoreType.DMA((3, 4))],
        2 * modes,
        19,
        in_specs=[HBM] * 4,
        limit=8,
    )
    def near(other, share, states, handed=()):
        signal, sums = states[:2]
        shapes = [real(signal.shape), real(sums.shape)]
        return call(
            functools.partial(near_terms, other, share),
            [signal, sums, residues, decays, skip_gain, *handed],
            shapes + [real(handed[0].shape)] if share == "lead" else shapes,
            [],
            10,
            7,
            aliases={5: 2} if share == "lead" else {5 + index: index for index in range(len(handed))},
        )

    *near_mine, total = near(False, "lead", mine, [mine[3]])
    near_mine = near(False, "rest", mine, near_mine)
    theirs = call(functools.partial(gather_states, True), [later_keys, later_values, decays], state_shapes, scratch, 2 * modes, 19)
    near_theirs = near(True, None, theirs)
    scratch = [shape for shape in (natural, real((SEG * (modes + 1), LANES)), table) for _ in range(PAIR)]
    operands_mine = [queries, *near_mine, mine[2], residues, decays]
    ahead = call(functools.partial(spread_ahead, False), operands_mine, half((rows, padded)), scratch, 2 * modes, 5)

    enter, reach = None, 1
    while reach < ctx_size:
        radix = min(4, ctx_size // reach)
        come = [lax.ppermute(total, "ctx", [(i, i ^ (turn * reach)) for i in range(ctx_size)]) for turn in TURNS[radix]]
        after = [near_theirs[0], ahead] if reach == 1 else []
        last = radix * reach == ctx_size
        result = call(
            functools.partial(carry, False, reach, radix, rows, len(after)),
            [decays, total, *after, *come] + ([] if enter is None else [enter]),
            [real((modes, count))] * (1 if last else 2),
            [],
            0,
            0,
        )
        enter, total = result[0], result[-1]
        reach *= radix
    enter_theirs = lax.ppermute(enter, "half", [(0, 1), (1, 0)])

    operands_theirs = [queries, *near_theirs, theirs[2], residues, decays]
    ahead_theirs = call(functools.partial(spread_ahead, True), [*operands_theirs, enter], half((rows, padded)), scratch, 2 * modes, 5)
    held = call(spread_mine, [*operands_mine, enter, ahead, ahead_theirs], half((rows, padded)), scratch, 2 * modes, 21, aliases={7: 0})
    mixed, _ = call(
        spread_and_store,
        [*operands_theirs, enter_theirs, held, ahead_theirs],
        [jax.ShapeDtypeStruct((rows, width), jnp.bfloat16), half((rows, padded))],
        scratch + [pltpu.SemaphoreType.DMA((blocks + 1,))],
        2 * modes,
        21,
        out_specs=[HBM, VMEM],
        aliases={8: 1},
    )
    return mixed


def solution(mesh):
    placed = (
        P("ctx", "chan"),
        P("ctx", "chan"),
        P("ctx", "chan"),
        P(None, "chan"),
        P(None, "chan"),
        P("chan"),
    )
    return jax.shard_map(shards, mesh=mesh, in_specs=placed, out_specs=P("ctx", "chan"), check_vma=False)
```

```python
import functools

import jax
import jax.numpy as jnp
from jax import lax
from jax.experimental import pallas as pl
from jax.experimental.pallas import tpu as pltpu
from jax.sharding import PartitionSpec as P

SEG = 8
CHUNK = 8
LANES = 128
SLABS = (0, 1, 2, 4)
PAIR = 2
AHEAD = 2
MIB = 2**20
TURNS = {2: (1,), 4: (2, 3, 1)}

VMEM = pl.BlockSpec(memory_space=pltpu.VMEM)
HBM = pl.BlockSpec(memory_space=pltpu.HBM)


def leads():
    origin = True
    for axis in ("chan", "half", "ctx"):
        origin = (lax.axis_index(axis) == 0) & origin
    return origin


def row(ref, index, lanes=slice(None)):
    return jnp.broadcast_to(ref[pl.ds(index, 1), lanes], (SEG, LANES))


def lane_block(block):
    return pl.ds(pl.multiple_of(block * LANES, LANES), LANES)


def channels_of(other, count):
    mine = lax.axis_index("half")
    return pl.multiple_of((1 - mine if other else mine) * count, LANES)


def near_tables(residue, decay, skip):
    term = residue * jnp.sqrt(decay)
    damp = jnp.exp(-decay)
    weight = term * damp
    taps = []
    for step in range(CHUNK):
        tap = jnp.sum(term, 0, keepdims=True)
        if step == 0:
            tap = tap + skip
        taps.append(jnp.broadcast_to(tap, (SEG, LANES)))
        term = term * damp
    return taps, weight


def near_sum(taps, signal, step):
    total = taps[0] * signal[step]
    for back in range(1, step + 1):
        total = total + taps[back] * signal[step - back]
    return total


def gather_states(other, key_ref, value_ref, decays_ref, signal_ref, sums_ref, scan_ref, *scratch, end_ref=None, arrive=None, near=None):
    rows = key_ref.shape[0]
    blocks, _, modes, _ = scan_ref.shape
    seg_len = rows // SEG
    chunks = seg_len // CHUNK
    pitch = seg_len + 1
    first = channels_of(other, blocks * LANES) if other else 0

    def one(block, natural, turned, damp, damp_chunk, *weights):
        lanes = lane_block(block)
        wide = pl.ds(pl.multiple_of(first + block * LANES, LANES), LANES)
        decay = decays_ref[:, wide]
        if near is not None:
            taps, weights[0][...] = near_tables(near[0][:, wide], decay, near[1][:, wide])
        damp[...] = jnp.exp(-decay)
        damp_chunk[...] = jnp.exp(-CHUNK * decay)
        damp_segment = jnp.exp(-seg_len * decay)
        for start in range(0, rows, 16):
            part = pl.ds(start, 16)
            place = start // seg_len * pitch + start % seg_len
            natural[pl.ds(place, 16), :] = key_ref[part, lanes].astype(jnp.float32) * value_ref[part, lanes].astype(jnp.float32)
        states = [None] * modes
        for chunk in range(chunks):
            signal = [natural[pl.ds(chunk * CHUNK + step, SEG, stride=pitch), :] for step in range(CHUNK)]
            for step in range(CHUNK):
                signal_ref[block, chunk * CHUNK + step] = signal[step] if near is None else near_sum(taps, signal, step)
            for mode in range(modes):
                factor = row(damp, mode)
                total = signal[0]
                for step in range(1, CHUNK):
                    total = total * factor + signal[step]
                if chunk < chunks - 1:
                    sums_ref[block, chunk, mode] = total if near is None else total * row(weights[0], mode)
                states[mode] = total if chunk == 0 else states[mode] * row(damp_chunk, mode) + total
        for mode in range(modes):
            turned[pl.ds(mode * (SEG + 1), SEG), :] = states[mode]
        state = jnp.zeros((modes, LANES), jnp.float32)
        for segment in range(SEG):
            scan_ref[block, segment] = state
            if end_ref is not None or segment < SEG - 1:
                state = state * damp_segment + turned[pl.ds(segment, modes, stride=SEG + 1), :]
        if end_ref is not None:
            end_ref[:, lanes] = state

    if arrive is not None:
        for turn in range(PAIR):
            arrive(turn)
            one(turn, *scratch[turn::PAIR])

    @pl.loop(0 if arrive is None else 1, blocks // PAIR)
    def _(pair):
        if arrive is not None:
            arrive(pair * PAIR)
        for turn in range(PAIR):
            one(pair * PAIR + turn, *scratch[turn::PAIR])


def gather_with_near(key_ref, value_ref, decays_ref, residues_ref, skip_ref, near_ref, scaled_ref, scan_ref, *scratch):
    gather_states(True, key_ref, value_ref, decays_ref, near_ref, scaled_ref, scan_ref, *scratch, near=(residues_ref, skip_ref))


def load_and_gather(
    key_ref, value_ref, query_ref, decays_ref, signal_ref, sums_ref, scan_ref, end_ref, later_key_ref, later_value_ref, later_query_ref, *scratch
):
    *scratch, keys, values, rates, sems = scratch
    blocks = scan_ref.shape[0]
    width = blocks * LANES
    first = channels_of(False, width)
    rate_copy = pltpu.make_async_copy(decays_ref.at[:, pl.ds(first, width)], rates, sems.at[2, 0])
    starts = [start for start in SLABS if start < blocks]
    slabs = []
    for index, (start, stop) in enumerate(zip(starts, starts[1:] + [blocks])):
        lanes = pl.ds(start * LANES, (stop - start) * LANES)
        wide = pl.ds(pl.multiple_of(first + start * LANES, LANES), (stop - start) * LANES)
        slabs.append(
            (
                pltpu.make_async_copy(key_ref.at[:, wide], keys.at[:, lanes], sems.at[0, index]),
                pltpu.make_async_copy(value_ref.at[:, wide], values.at[:, lanes], sems.at[1, index]),
            )
        )
        for copy in slabs[-1]:
            copy.start()
        if index == 0:
            rate_copy.start()
    later = pl.ds(channels_of(True, width), width)
    later_copies = (
        pltpu.make_async_copy(key_ref.at[:, later], later_key_ref.at[:, pl.ds(0, width)], sems.at[2, 1]),
        pltpu.make_async_copy(value_ref.at[:, later], later_value_ref.at[:, pl.ds(0, width)], sems.at[2, 2]),
        pltpu.make_async_copy(query_ref, later_query_ref.at[:, pl.ds(0, query_ref.shape[1])], sems.at[2, 3]),
    )
    for copy in later_copies:
        copy.start()
    rate_copy.wait()

    def arrive(block):
        for start, copies in zip(starts, slabs):

            @pl.when(block == start)
            def _(copies=copies):
                for copy in copies:
                    copy.wait()

    gather_states(False, keys, values, rates, signal_ref, sums_ref, scan_ref, *scratch, end_ref=end_ref, arrive=arrive)
    for copy in later_copies:
        copy.wait()


def carry(other, reach, radix, rows, after, decays_ref, total_ref, *refs):
    refs = list(refs[after:])
    come = {turn: refs.pop(0)[...] for turn in TURNS[radix]}
    come[0] = total_ref[...]
    enter = refs.pop(0)[...] if reach > 1 else 0.0
    count = total_ref.shape[1]
    decay = decays_ref[:, pl.ds(channels_of(other, count), count)]
    rank = lax.axis_index("ctx")
    digit = rank // reach & (radix - 1)
    inside = rank & (reach - 1)
    total = 0.0
    for turn in range(radix):
        source = digit ^ turn
        if turn:
            behind = jnp.maximum(digit - 1 - source, 0) * reach + inside
            enter = enter + jnp.where(source < digit, jnp.exp(-(behind * rows).astype(jnp.float32) * decay) * come[turn], 0.0)
        if len(refs) > 1:
            total = total + jnp.exp(-((radix - 1 - source) * (reach * rows)).astype(jnp.float32) * decay) * come[turn]
    refs[0][...] = enter
    if len(refs) > 1:
        refs[1][...] = total


def near_terms(share, signal_ref, sums_ref, residues_ref, decays_ref, skip_ref, *refs):
    near_ref, scaled_ref = refs[1:3] if share == "lead" else refs[-2:]
    blocks, steps, _, _ = signal_ref.shape
    modes = decays_ref.shape[0]
    chunks = steps // CHUNK
    first = channels_of(False, blocks * LANES)

    @pl.loop(0, jnp.where(leads() == (share == "lead"), blocks, 0))
    def _(block):
        wide = pl.ds(pl.multiple_of(first + block * LANES, LANES), LANES)
        taps, weight = near_tables(residues_ref[:, wide], decays_ref[:, wide], skip_ref[:, wide])
        for chunk in range(chunks):
            signal = [signal_ref[block, chunk * CHUNK + step] for step in range(CHUNK)]
            for step in range(CHUNK):
                near_ref[block, chunk * CHUNK + step] = near_sum(taps, signal, step)
        for mode in range(modes):
            factor = jnp.broadcast_to(weight[mode : mode + 1, :], (SEG, LANES))
            scaled = [factor * sums_ref[block, chunk, mode] for chunk in range(chunks - 1)]
            for chunk in range(chunks - 1):
                scaled_ref[block, chunk, mode] = scaled[chunk]


def spread_states(other, span, enter_ref, query_ref, near_ref, sums_ref, scan_ref, residues_ref, decays_ref, gated_ref, *scratch, leave=None):
    rows = gated_ref.shape[0]
    blocks, _, modes, _ = scan_ref.shape
    first = channels_of(other, blocks * LANES)
    seg_len = rows // SEG
    chunks = seg_len // CHUNK
    pitch = seg_len + 1

    def one(block, natural, turned, damp):
        lanes = lane_block(block)
        wide = pl.ds(pl.multiple_of(first + block * LANES, LANES), LANES)
        decay = decays_ref[:, wide]
        once = jnp.exp(-decay)
        damp[...] = once
        scale = residues_ref[:, wide] * jnp.sqrt(decay) * once
        damp_segment = jnp.exp(-seg_len * decay)
        enter = jnp.zeros((modes, LANES), jnp.float32) if enter_ref is None else enter_ref[:, lanes]
        for segment in range(SEG):
            turned[pl.ds(segment * (modes + 1), modes), :] = (scan_ref[block, segment] + enter) * scale
            enter = enter * damp_segment
        states = [turned[pl.ds(mode, SEG, stride=modes + 1), :] for mode in range(modes)]
        for chunk in range(chunks):
            conv = [near_ref[block, chunk * CHUNK + step] for step in range(CHUNK)]
            for mode in range(modes):
                factor = row(damp, mode)
                state = states[mode]
                for step in range(CHUNK):
                    conv[step] = conv[step] + state
                    if step < CHUNK - 1 or chunk < chunks - 1:
                        state = state * factor
                if chunk < chunks - 1:
                    states[mode] = state + sums_ref[block, chunk, mode]
            for step in range(CHUNK):
                natural[pl.ds(chunk * CHUNK + step, SEG, stride=pitch), :] = conv[step]
        for start in range(0, rows, 16):
            part = pl.ds(start, 16)
            place = start // seg_len * pitch + start % seg_len
            gated_ref[part, lanes] = (query_ref[part, wide].astype(jnp.float32) * natural[pl.ds(place, 16), :]).astype(jnp.bfloat16)

    @pl.loop(*span)
    def _(pair):
        for turn in range(PAIR):
            one(pair * PAIR + turn, *scratch[turn::PAIR])
        if leave is not None:
            for turn in range(PAIR):
                leave(pair * PAIR + turn)


def spread_ahead(other, query_ref, near_ref, sums_ref, scan_ref, residues_ref, decays_ref, *refs):
    gated_ref, *scratch = refs[1:] if other else refs
    span = 0, jnp.where(leads(), AHEAD, 0)
    spread_states(other, span, None, query_ref, near_ref, sums_ref, scan_ref, residues_ref, decays_ref, gated_ref, *scratch)


def spread_mine(query_ref, near_ref, sums_ref, scan_ref, residues_ref, decays_ref, enter_ref, *refs):
    gated_ref, *scratch = refs[2:]
    span = jnp.where(leads(), AHEAD, 0), scan_ref.shape[0] // PAIR
    spread_states(False, span, enter_ref, query_ref, near_ref, sums_ref, scan_ref, residues_ref, decays_ref, gated_ref, *scratch)


def spread_and_store(
    query_ref, near_ref, sums_ref, scan_ref, residues_ref, decays_ref, enter_ref, held_ref, _, mixed_ref, gated, *scratch
):
    *scratch, sems = scratch
    blocks = scan_ref.shape[0]
    width = blocks * LANES
    first = channels_of(True, width)
    held_copy = pltpu.make_async_copy(held_ref.at[:, pl.ds(0, width)], mixed_ref.at[:, pl.ds(channels_of(False, width), width)], sems.at[blocks])
    held_copy.start()

    def copy(block):
        wide = pl.ds(pl.multiple_of(first + block * LANES, LANES), LANES)
        return pltpu.make_async_copy(gated.at[:, lane_block(block)], mixed_ref.at[:, wide], sems.at[block])

    ahead = jnp.where(leads(), AHEAD, 0)

    @pl.loop(0, ahead * PAIR)
    def _(block):
        copy(block).start()

    spread_states(
        True,
        (ahead, blocks // PAIR),
        enter_ref,
        query_ref,
        near_ref,
        sums_ref,
        scan_ref,
        residues_ref,
        decays_ref,
        gated,
        *scratch,
        leave=lambda block: copy(block).start(),
    )

    @pl.loop(0, blocks)
    def _(block):
        copy(block).wait()

    held_copy.wait()


def shards(query_gate, key_gate, value_input, residues, decays, skip_gain):
    rows, width = key_gate.shape
    modes = residues.shape[0]
    seg_len = rows // SEG
    chunks = seg_len // CHUNK
    ctx_size = lax.axis_size("ctx")
    count = width // lax.axis_size("half")
    blocks = count // LANES
    padded = count + LANES * (1 - blocks % 2)
    skip_gain = skip_gain[None, :]
    real = functools.partial(pltpu.VMEM, dtype=jnp.float32)
    half = functools.partial(pltpu.VMEM, dtype=jnp.bfloat16)
    natural = real((SEG * (seg_len + 1), LANES))
    table = real((modes, LANES))

    def call(body, operands, out_shape, scratch, ops, moved, in_specs=None, out_specs=None, limit=4, aliases=None):
        return pl.pallas_call(
            body,
            in_specs=in_specs or [VMEM] * len(operands),
            out_specs=out_specs or jax.tree.map(lambda _: VMEM, out_shape),
            out_shape=out_shape,
            scratch_shapes=scratch,
            input_output_aliases=aliases or {},
            compiler_params=pltpu.CompilerParams(vmem_limit_bytes=limit * MIB),
            cost_estimate=pl.CostEstimate(flops=ops * rows * count, bytes_accessed=moved * rows * count, transcendentals=0),
            name=getattr(body, "func", body).__name__,
        )(*operands)

    state_shapes = [
        real((blocks, seg_len, SEG, LANES)),
        real((blocks, chunks - 1, modes, SEG, LANES)),
        real((blocks, SEG, modes, LANES)),
    ]
    scratch = [shape for shape in (natural, real((modes * (SEG + 1), LANES)), table, table) for _ in range(PAIR)]
    *mine, later_keys, later_values, queries = call(
        load_and_gather,
        [pltpu.with_memory_space_constraint(array, pltpu.HBM) for array in (key_gate, value_input, query_gate, decays)],
        state_shapes + [real((modes, count)), half((rows, padded)), half((rows, padded)), half((rows, width + LANES))],
        scratch + [half((rows, padded)), half((rows, padded)), real((modes, count)), pltpu.SemaphoreType.DMA((3, max(4, len(SLABS))))],
        2 * modes,
        19,
        in_specs=[HBM] * 4,
        limit=8,
    )
    def near(share, states, handed):
        signal, sums = states[:2]
        shapes = [real(signal.shape), real(sums.shape)]
        return call(
            functools.partial(near_terms, share),
            [signal, sums, residues, decays, skip_gain, *handed],
            shapes + [real(handed[0].shape)] if share == "lead" else shapes,
            [],
            10,
            7,
            aliases={5: 2} if share == "lead" else {5 + index: index for index in range(len(handed))},
        )

    *near_mine, total = near("lead", mine, [mine[3]])
    near_mine = near("rest", mine, near_mine)
    *near_theirs, scan_theirs = call(
        gather_with_near,
        [later_keys, later_values, decays, residues, skip_gain],
        state_shapes,
        scratch + [table] * PAIR,
        2 * modes,
        24,
    )
    scratch = [shape for shape in (natural, real((SEG * (modes + 1), LANES)), table) for _ in range(PAIR)]
    operands_mine = [queries, *near_mine, mine[2], residues, decays]
    ahead = call(functools.partial(spread_ahead, False), operands_mine, half((rows, padded)), scratch, 2 * modes, 5)

    enter, reach = None, 1
    while reach < ctx_size:
        radix = min(4, ctx_size // reach)
        come = [lax.ppermute(total, "ctx", [(i, i ^ (turn * reach)) for i in range(ctx_size)]) for turn in TURNS[radix]]
        after = [near_theirs[0], ahead] if reach == 1 else []
        last = radix * reach == ctx_size
        result = call(
            functools.partial(carry, False, reach, radix, rows, len(after)),
            [decays, total, *after, *come] + ([] if enter is None else [enter]),
            [real((modes, count))] * (1 if last else 2),
            [],
            0,
            0,
        )
        enter, total = result[0], result[-1]
        reach *= radix
    enter_theirs = lax.ppermute(enter, "half", [(0, 1), (1, 0)])

    operands_theirs = [queries, *near_theirs, scan_theirs, residues, decays]
    ahead_theirs = call(functools.partial(spread_ahead, True), [*operands_theirs, enter], half((rows, padded)), scratch, 2 * modes, 5)
    held = call(spread_mine, [*operands_mine, enter, ahead, ahead_theirs], half((rows, padded)), scratch, 2 * modes, 21, aliases={7: 0})
    mixed, _ = call(
        spread_and_store,
        [*operands_theirs, enter_theirs, held, ahead_theirs],
        [jax.ShapeDtypeStruct((rows, width), jnp.bfloat16), half((rows, padded))],
        scratch + [pltpu.SemaphoreType.DMA((blocks + 1,))],
        2 * modes,
        21,
        out_specs=[HBM, VMEM],
        aliases={8: 1},
    )
    return mixed


def solution(mesh):
    placed = (
        P("ctx", "chan"),
        P("ctx", "chan"),
        P("ctx", "chan"),
        P(None, "chan"),
        P(None, "chan"),
        P("chan"),
    )
    return jax.shard_map(shards, mesh=mesh, in_specs=placed, out_specs=P("ctx", "chan"), check_vma=False)
```

```python
import functools

import jax
import jax.numpy as jnp
from jax import lax
from jax.experimental import pallas as pl
from jax.experimental.pallas import tpu as pltpu
from jax.sharding import PartitionSpec as P

SEG = 8
CHUNK = 8
LANES = 128
SLABS = (0, 1, 2, 4)
PAIR = 2
AHEAD = 2
MIB = 2**20
TURNS = {2: (1,), 4: (2, 3, 1)}

VMEM = pl.BlockSpec(memory_space=pltpu.VMEM)
HBM = pl.BlockSpec(memory_space=pltpu.HBM)


def leads():
    origin = True
    for axis in ("chan", "half", "ctx"):
        origin = (lax.axis_index(axis) == 0) & origin
    return origin


def row(ref, index, lanes=slice(None)):
    return jnp.broadcast_to(ref[pl.ds(index, 1), lanes], (SEG, LANES))


def lane_block(block):
    return pl.ds(pl.multiple_of(block * LANES, LANES), LANES)


def channels_of(other, count):
    mine = lax.axis_index("half")
    return pl.multiple_of((1 - mine if other else mine) * count, LANES)


def near_tables(residue, decay, skip):
    term = residue * jnp.sqrt(decay)
    damp = jnp.exp(-decay)
    weight = term * damp
    taps = []
    for step in range(CHUNK):
        tap = jnp.sum(term, 0, keepdims=True)
        if step == 0:
            tap = tap + skip
        taps.append(jnp.broadcast_to(tap, (SEG, LANES)))
        term = term * damp
    return taps, weight


def near_sum(taps, signal, step):
    total = taps[0] * signal[step]
    for back in range(1, step + 1):
        total = total + taps[back] * signal[step - back]
    return total


def gather_states(other, key_ref, value_ref, decays_ref, signal_ref, sums_ref, scan_ref, *scratch, end_ref=None, arrive=None, near=None):
    rows = key_ref.shape[0]
    blocks, _, modes, _ = scan_ref.shape
    seg_len = rows // SEG
    chunks = seg_len // CHUNK
    pitch = seg_len + 1
    first = channels_of(other, blocks * LANES) if other else 0

    def one(block, natural, turned, damp, damp_chunk, *weights):
        lanes = lane_block(block)
        wide = pl.ds(pl.multiple_of(first + block * LANES, LANES), LANES)
        decay = decays_ref[:, wide]
        if near is not None:
            taps, weights[0][...] = near_tables(near[0][:, wide], decay, near[1][:, wide])
        damp[...] = jnp.exp(-decay)
        damp_chunk[...] = jnp.exp(-CHUNK * decay)
        damp_segment = jnp.exp(-seg_len * decay)
        for start in range(0, rows, 16):
            part = pl.ds(start, 16)
            place = start // seg_len * pitch + start % seg_len
            natural[pl.ds(place, 16), :] = key_ref[part, lanes].astype(jnp.float32) * value_ref[part, lanes].astype(jnp.float32)
        states = [None] * modes
        for chunk in range(chunks):
            signal = [natural[pl.ds(chunk * CHUNK + step, SEG, stride=pitch), :] for step in range(CHUNK)]
            for step in range(CHUNK):
                signal_ref[block, chunk * CHUNK + step] = signal[step] if near is None else near_sum(taps, signal, step)
            for mode in range(modes):
                factor = row(damp, mode)
                total = signal[0]
                for step in range(1, CHUNK):
                    total = total * factor + signal[step]
                if chunk < chunks - 1:
                    sums_ref[block, chunk, mode] = total if near is None else total * row(weights[0], mode)
                states[mode] = total if chunk == 0 else states[mode] * row(damp_chunk, mode) + total
        for mode in range(modes):
            turned[pl.ds(mode * (SEG + 1), SEG), :] = states[mode]
        state = jnp.zeros((modes, LANES), jnp.float32)
        for segment in range(SEG):
            scan_ref[block, segment] = state
            if end_ref is not None or segment < SEG - 1:
                state = state * damp_segment + turned[pl.ds(segment, modes, stride=SEG + 1), :]
        if end_ref is not None:
            end_ref[:, lanes] = state

    if arrive is not None:
        for turn in range(PAIR):
            arrive(turn)
            one(turn, *scratch[turn::PAIR])

    @pl.loop(0 if arrive is None else 1, blocks // PAIR)
    def _(pair):
        if arrive is not None:
            arrive(pair * PAIR)
        for turn in range(PAIR):
            one(pair * PAIR + turn, *scratch[turn::PAIR])


def gather_with_near(key_ref, value_ref, decays_ref, residues_ref, skip_ref, near_ref, scaled_ref, scan_ref, *scratch):
    gather_states(True, key_ref, value_ref, decays_ref, near_ref, scaled_ref, scan_ref, *scratch, near=(residues_ref, skip_ref))


def load_and_gather(
    key_ref, value_ref, query_ref, decays_ref, signal_ref, sums_ref, scan_ref, end_ref, later_key_ref, later_value_ref, later_query_ref, *scratch
):
    *scratch, keys, values, rates, sems = scratch
    blocks = scan_ref.shape[0]
    width = blocks * LANES
    first = channels_of(False, width)
    rate_copy = pltpu.make_async_copy(decays_ref.at[:, pl.ds(first, width)], rates, sems.at[2, 0])
    starts = [start for start in SLABS if start < blocks]
    slabs = []
    for index, (start, stop) in enumerate(zip(starts, starts[1:] + [blocks])):
        lanes = pl.ds(start * LANES, (stop - start) * LANES)
        wide = pl.ds(pl.multiple_of(first + start * LANES, LANES), (stop - start) * LANES)
        slabs.append(
            (
                pltpu.make_async_copy(key_ref.at[:, wide], keys.at[:, lanes], sems.at[0, index]),
                pltpu.make_async_copy(value_ref.at[:, wide], values.at[:, lanes], sems.at[1, index]),
            )
        )
        for copy in slabs[-1]:
            copy.start()
        if index == 0:
            rate_copy.start()
    later = pl.ds(channels_of(True, width), width)
    later_copies = (
        pltpu.make_async_copy(key_ref.at[:, later], later_key_ref.at[:, pl.ds(0, width)], sems.at[2, 1]),
        pltpu.make_async_copy(value_ref.at[:, later], later_value_ref.at[:, pl.ds(0, width)], sems.at[2, 2]),
        pltpu.make_async_copy(query_ref, later_query_ref.at[:, pl.ds(0, query_ref.shape[1])], sems.at[2, 3]),
    )
    for copy in later_copies:
        copy.start()
    rate_copy.wait()

    def arrive(block):
        for start, copies in zip(starts, slabs):

            @pl.when(block == start)
            def _(copies=copies):
                for copy in copies:
                    copy.wait()

    gather_states(False, keys, values, rates, signal_ref, sums_ref, scan_ref, *scratch, end_ref=end_ref, arrive=arrive)
    for copy in later_copies:
        copy.wait()


def carry(other, reach, radix, rows, after, decays_ref, total_ref, *refs):
    refs = list(refs[after:])
    come = {turn: refs.pop(0)[...] for turn in TURNS[radix]}
    come[0] = total_ref[...]
    enter = refs.pop(0)[...] if reach > 1 else 0.0
    count = total_ref.shape[1]
    decay = decays_ref[:, pl.ds(channels_of(other, count), count)]
    rank = lax.axis_index("ctx")
    digit = rank // reach & (radix - 1)
    inside = rank & (reach - 1)
    total = 0.0
    for turn in range(radix):
        source = digit ^ turn
        if turn:
            behind = jnp.maximum(digit - 1 - source, 0) * reach + inside
            enter = enter + jnp.where(source < digit, jnp.exp(-(behind * rows).astype(jnp.float32) * decay) * come[turn], 0.0)
        if len(refs) > 1:
            total = total + jnp.exp(-((radix - 1 - source) * (reach * rows)).astype(jnp.float32) * decay) * come[turn]
    refs[0][...] = enter
    if len(refs) > 1:
        refs[1][...] = total


def near_terms(share, signal_ref, sums_ref, residues_ref, decays_ref, skip_ref, *refs):
    near_ref, scaled_ref = refs[1:3] if share == "lead" else refs[-2:]
    blocks, steps, _, _ = signal_ref.shape
    modes = decays_ref.shape[0]
    chunks = steps // CHUNK
    first = channels_of(False, blocks * LANES)

    @pl.loop(0, jnp.where(leads() == (share == "lead"), blocks, 0))
    def _(block):
        wide = pl.ds(pl.multiple_of(first + block * LANES, LANES), LANES)
        taps, weight = near_tables(residues_ref[:, wide], decays_ref[:, wide], skip_ref[:, wide])
        for chunk in range(chunks):
            signal = [signal_ref[block, chunk * CHUNK + step] for step in range(CHUNK)]
            for step in range(CHUNK):
                near_ref[block, chunk * CHUNK + step] = near_sum(taps, signal, step)
        for mode in range(modes):
            factor = jnp.broadcast_to(weight[mode : mode + 1, :], (SEG, LANES))
            scaled = [factor * sums_ref[block, chunk, mode] for chunk in range(chunks - 1)]
            for chunk in range(chunks - 1):
                scaled_ref[block, chunk, mode] = scaled[chunk]


def spread_states(other, span, enter_ref, query_ref, near_ref, sums_ref, scan_ref, residues_ref, decays_ref, gated_ref, *scratch, leave=None):
    rows = gated_ref.shape[0]
    blocks, _, modes, _ = scan_ref.shape
    first = channels_of(other, blocks * LANES)
    seg_len = rows // SEG
    chunks = seg_len // CHUNK
    pitch = seg_len + 1

    def one(block, natural, turned, damp):
        lanes = lane_block(block)
        wide = pl.ds(pl.multiple_of(first + block * LANES, LANES), LANES)
        decay = decays_ref[:, wide]
        once = jnp.exp(-decay)
        damp[...] = once
        scale = residues_ref[:, wide] * jnp.sqrt(decay) * once
        damp_segment = jnp.exp(-seg_len * decay)
        enter = jnp.zeros((modes, LANES), jnp.float32) if enter_ref is None else enter_ref[:, lanes]
        for segment in range(SEG):
            turned[pl.ds(segment * (modes + 1), modes), :] = (scan_ref[block, segment] + enter) * scale
            enter = enter * damp_segment
        states = [turned[pl.ds(mode, SEG, stride=modes + 1), :] for mode in range(modes)]
        for chunk in range(chunks):
            conv = [near_ref[block, chunk * CHUNK + step] for step in range(CHUNK)]
            for mode in range(modes):
                factor = row(damp, mode)
                state = states[mode]
                for step in range(CHUNK):
                    conv[step] = conv[step] + state
                    if step < CHUNK - 1 or chunk < chunks - 1:
                        state = state * factor
                if chunk < chunks - 1:
                    states[mode] = state + sums_ref[block, chunk, mode]
            for step in range(CHUNK):
                natural[pl.ds(chunk * CHUNK + step, SEG, stride=pitch), :] = conv[step]
        for start in range(0, rows, 16):
            part = pl.ds(start, 16)
            place = start // seg_len * pitch + start % seg_len
            gated_ref[part, lanes] = (query_ref[part, wide].astype(jnp.float32) * natural[pl.ds(place, 16), :]).astype(jnp.bfloat16)

    @pl.loop(*span)
    def _(pair):
        for turn in range(PAIR):
            one(pair * PAIR + turn, *scratch[turn::PAIR])
            if leave is not None:
                leave(pair * PAIR + turn)


def spread_ahead(other, query_ref, near_ref, sums_ref, scan_ref, residues_ref, decays_ref, *refs):
    gated_ref, *scratch = refs[1:] if other else refs
    span = 0, jnp.where(leads(), AHEAD, 0)
    spread_states(other, span, None, query_ref, near_ref, sums_ref, scan_ref, residues_ref, decays_ref, gated_ref, *scratch)


def spread_mine(query_ref, near_ref, sums_ref, scan_ref, residues_ref, decays_ref, enter_ref, *refs):
    gated_ref, *scratch = refs[2:]
    span = jnp.where(leads(), AHEAD, 0), scan_ref.shape[0] // PAIR
    spread_states(False, span, enter_ref, query_ref, near_ref, sums_ref, scan_ref, residues_ref, decays_ref, gated_ref, *scratch)


def spread_and_store(
    query_ref, near_ref, sums_ref, scan_ref, residues_ref, decays_ref, enter_ref, held_ref, _, mixed_ref, gated, *scratch
):
    *scratch, sems = scratch
    blocks = scan_ref.shape[0]
    width = blocks * LANES
    first = channels_of(True, width)
    held_copy = pltpu.make_async_copy(held_ref.at[:, pl.ds(0, width)], mixed_ref.at[:, pl.ds(channels_of(False, width), width)], sems.at[blocks])
    held_copy.start()

    def copy(block):
        wide = pl.ds(pl.multiple_of(first + block * LANES, LANES), LANES)
        return pltpu.make_async_copy(gated.at[:, lane_block(block)], mixed_ref.at[:, wide], sems.at[block])

    ahead = jnp.where(leads(), AHEAD, 0)

    @pl.loop(0, ahead * PAIR)
    def _(block):
        copy(block).start()

    spread_states(
        True,
        (ahead, blocks // PAIR),
        enter_ref,
        query_ref,
        near_ref,
        sums_ref,
        scan_ref,
        residues_ref,
        decays_ref,
        gated,
        *scratch,
        leave=lambda block: copy(block).start(),
    )

    @pl.loop(0, blocks)
    def _(block):
        copy(block).wait()

    held_copy.wait()


def shards(query_gate, key_gate, value_input, residues, decays, skip_gain):
    rows, width = key_gate.shape
    modes = residues.shape[0]
    seg_len = rows // SEG
    chunks = seg_len // CHUNK
    ctx_size = lax.axis_size("ctx")
    count = width // lax.axis_size("half")
    blocks = count // LANES
    padded = count + LANES * (1 - blocks % 2)
    skip_gain = skip_gain[None, :]
    real = functools.partial(pltpu.VMEM, dtype=jnp.float32)
    half = functools.partial(pltpu.VMEM, dtype=jnp.bfloat16)
    natural = real((SEG * (seg_len + 1), LANES))
    table = real((modes, LANES))

    def call(body, operands, out_shape, scratch, ops, moved, in_specs=None, out_specs=None, limit=4, aliases=None):
        return pl.pallas_call(
            body,
            in_specs=in_specs or [VMEM] * len(operands),
            out_specs=out_specs or jax.tree.map(lambda _: VMEM, out_shape),
            out_shape=out_shape,
            scratch_shapes=scratch,
            input_output_aliases=aliases or {},
            compiler_params=pltpu.CompilerParams(vmem_limit_bytes=limit * MIB),
            cost_estimate=pl.CostEstimate(flops=ops * rows * count, bytes_accessed=moved * rows * count, transcendentals=0),
            name=getattr(body, "func", body).__name__,
        )(*operands)

    state_shapes = [
        real((blocks, seg_len, SEG, LANES)),
        real((blocks, chunks - 1, modes, SEG, LANES)),
        real((blocks, SEG, modes, LANES)),
    ]
    scratch = [shape for shape in (natural, real((modes * (SEG + 1), LANES)), table, table) for _ in range(PAIR)]
    *mine, later_keys, later_values, queries = call(
        load_and_gather,
        [pltpu.with_memory_space_constraint(array, pltpu.HBM) for array in (key_gate, value_input, query_gate, decays)],
        state_shapes + [real((modes, count)), half((rows, padded)), half((rows, padded)), half((rows, width + LANES))],
        scratch + [half((rows, padded)), half((rows, padded)), real((modes, count)), pltpu.SemaphoreType.DMA((3, max(4, len(SLABS))))],
        2 * modes,
        19,
        in_specs=[HBM] * 4,
        limit=8,
    )
    def near(share, states, handed):
        signal, sums = states[:2]
        shapes = [real(signal.shape), real(sums.shape)]
        return call(
            functools.partial(near_terms, share),
            [signal, sums, residues, decays, skip_gain, *handed],
            shapes + [real(handed[0].shape)] if share == "lead" else shapes,
            [],
            10,
            7,
            aliases={5: 2} if share == "lead" else {5 + index: index for index in range(len(handed))},
        )

    *near_mine, total = near("lead", mine, [mine[3]])
    near_mine = near("rest", mine, near_mine)
    *near_theirs, scan_theirs = call(
        gather_with_near,
        [later_keys, later_values, decays, residues, skip_gain],
        state_shapes,
        scratch + [table] * PAIR,
        2 * modes,
        24,
    )
    scratch = [shape for shape in (natural, real((SEG * (modes + 1), LANES)), table) for _ in range(PAIR)]
    operands_mine = [queries, *near_mine, mine[2], residues, decays]
    ahead = call(functools.partial(spread_ahead, False), operands_mine, half((rows, padded)), scratch, 2 * modes, 5)

    enter, reach = None, 1
    while reach < ctx_size:
        radix = min(4, ctx_size // reach)
        come = [lax.ppermute(total, "ctx", [(i, i ^ (turn * reach)) for i in range(ctx_size)]) for turn in TURNS[radix]]
        after = [near_theirs[0], ahead] if reach == 1 else []
        last = radix * reach == ctx_size
        result = call(
            functools.partial(carry, False, reach, radix, rows, len(after)),
            [decays, total, *after, *come] + ([] if enter is None else [enter]),
            [real((modes, count))] * (1 if last else 2),
            [],
            0,
            0,
        )
        enter, total = result[0], result[-1]
        reach *= radix
    enter_theirs = lax.ppermute(enter, "half", [(0, 1), (1, 0)])

    operands_theirs = [queries, *near_theirs, scan_theirs, residues, decays]
    ahead_theirs = call(functools.partial(spread_ahead, True), [*operands_theirs, enter], half((rows, padded)), scratch, 2 * modes, 5)
    held = call(spread_mine, [*operands_mine, enter, ahead, ahead_theirs], half((rows, padded)), scratch, 2 * modes, 21, aliases={7: 0})
    mixed, _ = call(
        spread_and_store,
        [*operands_theirs, enter_theirs, held, ahead_theirs],
        [jax.ShapeDtypeStruct((rows, width), jnp.bfloat16), half((rows, padded))],
        scratch + [pltpu.SemaphoreType.DMA((blocks + 1,))],
        2 * modes,
        21,
        out_specs=[HBM, VMEM],
        aliases={8: 1},
    )
    return mixed


def solution(mesh):
    placed = (
        P("ctx", "chan"),
        P("ctx", "chan"),
        P("ctx", "chan"),
        P(None, "chan"),
        P(None, "chan"),
        P("chan"),
    )
    return jax.shard_map(shards, mesh=mesh, in_specs=placed, out_specs=P("ctx", "chan"), check_vma=False)
```

```python
import functools

import jax
import jax.numpy as jnp
from jax import lax
from jax.experimental import pallas as pl
from jax.experimental.pallas import tpu as pltpu
from jax.sharding import PartitionSpec as P

SEG = 8
CHUNK = 8
LANES = 128
SLABS = (0, 1, 2, 4)
PAIR = 4
AHEAD = 1
MIB = 2**20
TURNS = {2: (1,), 4: (2, 3, 1)}

VMEM = pl.BlockSpec(memory_space=pltpu.VMEM)
HBM = pl.BlockSpec(memory_space=pltpu.HBM)


def leads():
    origin = True
    for axis in ("chan", "half", "ctx"):
        origin = (lax.axis_index(axis) == 0) & origin
    return origin


def row(ref, index, lanes=slice(None)):
    return jnp.broadcast_to(ref[pl.ds(index, 1), lanes], (SEG, LANES))


def lane_block(block):
    return pl.ds(pl.multiple_of(block * LANES, LANES), LANES)


def channels_of(other, count):
    mine = lax.axis_index("half")
    return pl.multiple_of((1 - mine if other else mine) * count, LANES)


def near_tables(residue, decay, skip):
    term = residue * jnp.sqrt(decay)
    damp = jnp.exp(-decay)
    weight = term * damp
    taps = []
    for step in range(CHUNK):
        tap = jnp.sum(term, 0, keepdims=True)
        if step == 0:
            tap = tap + skip
        taps.append(jnp.broadcast_to(tap, (SEG, LANES)))
        term = term * damp
    return taps, weight


def near_sum(taps, signal, step):
    total = taps[0] * signal[step]
    for back in range(1, step + 1):
        total = total + taps[back] * signal[step - back]
    return total


def gather_states(other, key_ref, value_ref, decays_ref, signal_ref, sums_ref, scan_ref, *scratch, end_ref=None, arrive=None, near=None):
    rows = key_ref.shape[0]
    blocks, _, modes, _ = scan_ref.shape
    seg_len = rows // SEG
    chunks = seg_len // CHUNK
    pitch = seg_len + 1
    first = channels_of(other, blocks * LANES) if other else 0

    def one(block, natural, turned, damp, damp_chunk, *weights):
        lanes = lane_block(block)
        wide = pl.ds(pl.multiple_of(first + block * LANES, LANES), LANES)
        decay = decays_ref[:, wide]
        if near is not None:
            taps, weights[0][...] = near_tables(near[0][:, wide], decay, near[1][:, wide])
        damp[...] = jnp.exp(-decay)
        damp_chunk[...] = jnp.exp(-CHUNK * decay)
        damp_segment = jnp.exp(-seg_len * decay)
        for start in range(0, rows, 16):
            part = pl.ds(start, 16)
            place = start // seg_len * pitch + start % seg_len
            natural[pl.ds(place, 16), :] = key_ref[part, lanes].astype(jnp.float32) * value_ref[part, lanes].astype(jnp.float32)
        states = [None] * modes
        for chunk in range(chunks):
            signal = [natural[pl.ds(chunk * CHUNK + step, SEG, stride=pitch), :] for step in range(CHUNK)]
            for step in range(CHUNK):
                signal_ref[block, chunk * CHUNK + step] = signal[step] if near is None else near_sum(taps, signal, step)
            for mode in range(modes):
                factor = row(damp, mode)
                total = signal[0]
                for step in range(1, CHUNK):
                    total = total * factor + signal[step]
                if chunk < chunks - 1:
                    sums_ref[block, chunk, mode] = total if near is None else total * row(weights[0], mode)
                states[mode] = total if chunk == 0 else states[mode] * row(damp_chunk, mode) + total
        for mode in range(modes):
            turned[pl.ds(mode * (SEG + 1), SEG), :] = states[mode]
        state = jnp.zeros((modes, LANES), jnp.float32)
        for segment in range(SEG):
            scan_ref[block, segment] = state
            if end_ref is not None or segment < SEG - 1:
                state = state * damp_segment + turned[pl.ds(segment, modes, stride=SEG + 1), :]
        if end_ref is not None:
            end_ref[:, lanes] = state

    if arrive is not None:
        for turn in range(PAIR):
            arrive(turn)
            one(turn, *scratch[turn::PAIR])

    @pl.loop(0 if arrive is None else 1, blocks // PAIR)
    def _(pair):
        if arrive is not None:
            arrive(pair * PAIR)
        for turn in range(PAIR):
            one(pair * PAIR + turn, *scratch[turn::PAIR])


def gather_with_near(key_ref, value_ref, decays_ref, residues_ref, skip_ref, near_ref, scaled_ref, scan_ref, *scratch):
    gather_states(True, key_ref, value_ref, decays_ref, near_ref, scaled_ref, scan_ref, *scratch, near=(residues_ref, skip_ref))


def load_and_gather(
    key_ref, value_ref, query_ref, decays_ref, signal_ref, sums_ref, scan_ref, end_ref, later_key_ref, later_value_ref, later_query_ref, *scratch
):
    *scratch, keys, values, rates, sems = scratch
    blocks = scan_ref.shape[0]
    width = blocks * LANES
    first = channels_of(False, width)
    rate_copy = pltpu.make_async_copy(decays_ref.at[:, pl.ds(first, width)], rates, sems.at[2, 0])
    starts = [start for start in SLABS if start < blocks]
    slabs = []
    for index, (start, stop) in enumerate(zip(starts, starts[1:] + [blocks])):
        lanes = pl.ds(start * LANES, (stop - start) * LANES)
        wide = pl.ds(pl.multiple_of(first + start * LANES, LANES), (stop - start) * LANES)
        slabs.append(
            (
                pltpu.make_async_copy(key_ref.at[:, wide], keys.at[:, lanes], sems.at[0, index]),
                pltpu.make_async_copy(value_ref.at[:, wide], values.at[:, lanes], sems.at[1, index]),
            )
        )
        for copy in slabs[-1]:
            copy.start()
        if index == 0:
            rate_copy.start()
    later = pl.ds(channels_of(True, width), width)
    later_copies = (
        pltpu.make_async_copy(key_ref.at[:, later], later_key_ref.at[:, pl.ds(0, width)], sems.at[2, 1]),
        pltpu.make_async_copy(value_ref.at[:, later], later_value_ref.at[:, pl.ds(0, width)], sems.at[2, 2]),
        pltpu.make_async_copy(query_ref, later_query_ref.at[:, pl.ds(0, query_ref.shape[1])], sems.at[2, 3]),
    )
    for copy in later_copies:
        copy.start()
    rate_copy.wait()

    def arrive(block):
        for start, copies in zip(starts, slabs):

            @pl.when(block == start)
            def _(copies=copies):
                for copy in copies:
                    copy.wait()

    gather_states(False, keys, values, rates, signal_ref, sums_ref, scan_ref, *scratch, end_ref=end_ref, arrive=arrive)
    for copy in later_copies:
        copy.wait()


def carry(other, reach, radix, rows, after, decays_ref, total_ref, *refs):
    refs = list(refs[after:])
    come = {turn: refs.pop(0)[...] for turn in TURNS[radix]}
    come[0] = total_ref[...]
    enter = refs.pop(0)[...] if reach > 1 else 0.0
    count = total_ref.shape[1]
    decay = decays_ref[:, pl.ds(channels_of(other, count), count)]
    rank = lax.axis_index("ctx")
    digit = rank // reach & (radix - 1)
    inside = rank & (reach - 1)
    total = 0.0
    for turn in range(radix):
        source = digit ^ turn
        if turn:
            behind = jnp.maximum(digit - 1 - source, 0) * reach + inside
            enter = enter + jnp.where(source < digit, jnp.exp(-(behind * rows).astype(jnp.float32) * decay) * come[turn], 0.0)
        if len(refs) > 1:
            total = total + jnp.exp(-((radix - 1 - source) * (reach * rows)).astype(jnp.float32) * decay) * come[turn]
    refs[0][...] = enter
    if len(refs) > 1:
        refs[1][...] = total


def near_terms(share, signal_ref, sums_ref, residues_ref, decays_ref, skip_ref, *refs):
    near_ref, scaled_ref = refs[1:3] if share == "lead" else refs[-2:]
    blocks, steps, _, _ = signal_ref.shape
    modes = decays_ref.shape[0]
    chunks = steps // CHUNK
    first = channels_of(False, blocks * LANES)

    @pl.loop(0, jnp.where(leads() == (share == "lead"), blocks, 0))
    def _(block):
        wide = pl.ds(pl.multiple_of(first + block * LANES, LANES), LANES)
        taps, weight = near_tables(residues_ref[:, wide], decays_ref[:, wide], skip_ref[:, wide])
        for chunk in range(chunks):
            signal = [signal_ref[block, chunk * CHUNK + step] for step in range(CHUNK)]
            for step in range(CHUNK):
                near_ref[block, chunk * CHUNK + step] = near_sum(taps, signal, step)
        for mode in range(modes):
            factor = jnp.broadcast_to(weight[mode : mode + 1, :], (SEG, LANES))
            scaled = [factor * sums_ref[block, chunk, mode] for chunk in range(chunks - 1)]
            for chunk in range(chunks - 1):
                scaled_ref[block, chunk, mode] = scaled[chunk]


def spread_states(other, span, enter_ref, query_ref, near_ref, sums_ref, scan_ref, residues_ref, decays_ref, gated_ref, *scratch, leave=None):
    rows = gated_ref.shape[0]
    blocks, _, modes, _ = scan_ref.shape
    first = channels_of(other, blocks * LANES)
    seg_len = rows // SEG
    chunks = seg_len // CHUNK
    pitch = seg_len + 1

    def one(block, natural, turned, damp):
        lanes = lane_block(block)
        wide = pl.ds(pl.multiple_of(first + block * LANES, LANES), LANES)
        decay = decays_ref[:, wide]
        once = jnp.exp(-decay)
        damp[...] = once
        scale = residues_ref[:, wide] * jnp.sqrt(decay) * once
        damp_segment = jnp.exp(-seg_len * decay)
        enter = jnp.zeros((modes, LANES), jnp.float32) if enter_ref is None else enter_ref[:, lanes]
        for segment in range(SEG):
            turned[pl.ds(segment * (modes + 1), modes), :] = (scan_ref[block, segment] + enter) * scale
            enter = enter * damp_segment
        states = [turned[pl.ds(mode, SEG, stride=modes + 1), :] for mode in range(modes)]
        for chunk in range(chunks):
            conv = [near_ref[block, chunk * CHUNK + step] for step in range(CHUNK)]
            for mode in range(modes):
                factor = row(damp, mode)
                state = states[mode]
                for step in range(CHUNK):
                    conv[step] = conv[step] + state
                    if step < CHUNK - 1 or chunk < chunks - 1:
                        state = state * factor
                if chunk < chunks - 1:
                    states[mode] = state + sums_ref[block, chunk, mode]
            for step in range(CHUNK):
                natural[pl.ds(chunk * CHUNK + step, SEG, stride=pitch), :] = conv[step]
        for start in range(0, rows, 16):
            part = pl.ds(start, 16)
            place = start // seg_len * pitch + start % seg_len
            gated_ref[part, lanes] = (query_ref[part, wide].astype(jnp.float32) * natural[pl.ds(place, 16), :]).astype(jnp.bfloat16)

    @pl.loop(*span)
    def _(pair):
        for turn in range(PAIR):
            one(pair * PAIR + turn, *scratch[turn::PAIR])
            if leave is not None:
                leave(pair * PAIR + turn)


def spread_ahead(other, query_ref, near_ref, sums_ref, scan_ref, residues_ref, decays_ref, *refs):
    gated_ref, *scratch = refs[1:] if other else refs
    span = 0, jnp.where(leads(), AHEAD, 0)
    spread_states(other, span, None, query_ref, near_ref, sums_ref, scan_ref, residues_ref, decays_ref, gated_ref, *scratch)


def spread_mine(query_ref, near_ref, sums_ref, scan_ref, residues_ref, decays_ref, enter_ref, *refs):
    gated_ref, *scratch = refs[2:]
    span = jnp.where(leads(), AHEAD, 0), scan_ref.shape[0] // PAIR
    spread_states(False, span, enter_ref, query_ref, near_ref, sums_ref, scan_ref, residues_ref, decays_ref, gated_ref, *scratch)


def spread_and_store(
    query_ref, near_ref, sums_ref, scan_ref, residues_ref, decays_ref, enter_ref, held_ref, _, mixed_ref, gated, *scratch
):
    *scratch, sems = scratch
    blocks = scan_ref.shape[0]
    width = blocks * LANES
    first = channels_of(True, width)
    held_copy = pltpu.make_async_copy(held_ref.at[:, pl.ds(0, width)], mixed_ref.at[:, pl.ds(channels_of(False, width), width)], sems.at[blocks])
    held_copy.start()

    def copy(block):
        wide = pl.ds(pl.multiple_of(first + block * LANES, LANES), LANES)
        return pltpu.make_async_copy(gated.at[:, lane_block(block)], mixed_ref.at[:, wide], sems.at[block])

    ahead = jnp.where(leads(), AHEAD, 0)

    @pl.loop(0, ahead * PAIR)
    def _(block):
        copy(block).start()

    spread_states(
        True,
        (ahead, blocks // PAIR),
        enter_ref,
        query_ref,
        near_ref,
        sums_ref,
        scan_ref,
        residues_ref,
        decays_ref,
        gated,
        *scratch,
        leave=lambda block: copy(block).start(),
    )

    @pl.loop(0, blocks)
    def _(block):
        copy(block).wait()

    held_copy.wait()


def shards(query_gate, key_gate, value_input, residues, decays, skip_gain):
    rows, width = key_gate.shape
    modes = residues.shape[0]
    seg_len = rows // SEG
    chunks = seg_len // CHUNK
    ctx_size = lax.axis_size("ctx")
    count = width // lax.axis_size("half")
    blocks = count // LANES
    padded = count + LANES * (1 - blocks % 2)
    skip_gain = skip_gain[None, :]
    real = functools.partial(pltpu.VMEM, dtype=jnp.float32)
    half = functools.partial(pltpu.VMEM, dtype=jnp.bfloat16)
    natural = real((SEG * (seg_len + 1), LANES))
    table = real((modes, LANES))

    def call(body, operands, out_shape, scratch, ops, moved, in_specs=None, out_specs=None, limit=4, aliases=None):
        return pl.pallas_call(
            body,
            in_specs=in_specs or [VMEM] * len(operands),
            out_specs=out_specs or jax.tree.map(lambda _: VMEM, out_shape),
            out_shape=out_shape,
            scratch_shapes=scratch,
            input_output_aliases=aliases or {},
            compiler_params=pltpu.CompilerParams(vmem_limit_bytes=limit * MIB),
            cost_estimate=pl.CostEstimate(flops=ops * rows * count, bytes_accessed=moved * rows * count, transcendentals=0),
            name=getattr(body, "func", body).__name__,
        )(*operands)

    state_shapes = [
        real((blocks, seg_len, SEG, LANES)),
        real((blocks, chunks - 1, modes, SEG, LANES)),
        real((blocks, SEG, modes, LANES)),
    ]
    scratch = [shape for shape in (natural, real((modes * (SEG + 1), LANES)), table, table) for _ in range(PAIR)]
    *mine, later_keys, later_values, queries = call(
        load_and_gather,
        [pltpu.with_memory_space_constraint(array, pltpu.HBM) for array in (key_gate, value_input, query_gate, decays)],
        state_shapes + [real((modes, count)), half((rows, padded)), half((rows, padded)), half((rows, width + LANES))],
        scratch + [half((rows, padded)), half((rows, padded)), real((modes, count)), pltpu.SemaphoreType.DMA((3, max(4, len(SLABS))))],
        2 * modes,
        19,
        in_specs=[HBM] * 4,
        limit=8,
    )
    def near(share, states, handed):
        signal, sums = states[:2]
        shapes = [real(signal.shape), real(sums.shape)]
        return call(
            functools.partial(near_terms, share),
            [signal, sums, residues, decays, skip_gain, *handed],
            shapes + [real(handed[0].shape)] if share == "lead" else shapes,
            [],
            10,
            7,
            aliases={5: 2} if share == "lead" else {5 + index: index for index in range(len(handed))},
        )

    *near_mine, total = near("lead", mine, [mine[3]])
    near_mine = near("rest", mine, near_mine)
    *near_theirs, scan_theirs = call(
        gather_with_near,
        [later_keys, later_values, decays, residues, skip_gain],
        state_shapes,
        scratch + [table] * PAIR,
        2 * modes,
        24,
    )
    scratch = [shape for shape in (natural, real((SEG * (modes + 1), LANES)), table) for _ in range(PAIR)]
    operands_mine = [queries, *near_mine, mine[2], residues, decays]
    ahead = call(functools.partial(spread_ahead, False), operands_mine, half((rows, padded)), scratch, 2 * modes, 5)

    enter, reach = None, 1
    while reach < ctx_size:
        radix = min(4, ctx_size // reach)
        come = [lax.ppermute(total, "ctx", [(i, i ^ (turn * reach)) for i in range(ctx_size)]) for turn in TURNS[radix]]
        after = [near_theirs[0], ahead] if reach == 1 else []
        last = radix * reach == ctx_size
        result = call(
            functools.partial(carry, False, reach, radix, rows, len(after)),
            [decays, total, *after, *come] + ([] if enter is None else [enter]),
            [real((modes, count))] * (1 if last else 2),
            [],
            0,
            0,
        )
        enter, total = result[0], result[-1]
        reach *= radix
    enter_theirs = lax.ppermute(enter, "half", [(0, 1), (1, 0)])

    operands_theirs = [queries, *near_theirs, scan_theirs, residues, decays]
    ahead_theirs = call(functools.partial(spread_ahead, True), [*operands_theirs, enter], half((rows, padded)), scratch, 2 * modes, 5)
    held = call(spread_mine, [*operands_mine, enter, ahead, ahead_theirs], half((rows, padded)), scratch, 2 * modes, 21, aliases={7: 0})
    mixed, _ = call(
        spread_and_store,
        [*operands_theirs, enter_theirs, held, ahead_theirs],
        [jax.ShapeDtypeStruct((rows, width), jnp.bfloat16), half((rows, padded))],
        scratch + [pltpu.SemaphoreType.DMA((blocks + 1,))],
        2 * modes,
        21,
        out_specs=[HBM, VMEM],
        aliases={8: 1},
    )
    return mixed


def solution(mesh):
    placed = (
        P("ctx", "chan"),
        P("ctx", "chan"),
        P("ctx", "chan"),
        P(None, "chan"),
        P(None, "chan"),
        P("chan"),
    )
    return jax.shard_map(shards, mesh=mesh, in_specs=placed, out_specs=P("ctx", "chan"), check_vma=False)
```
